256 devices in a mesh: dp: 32 (over y_lo, z, core), rows: 8 (over y_hi, x).
Axes of the slice: x: 4, y: 4 (y_hi: 2, y_lo: 2; y = y_hi * 2 + y_lo), z: 8, core: 2. Of those that a mesh axis runs over, the one named last changes fastest.
Arguments:
- block_input: bfloat16 [64, 48, 48, 768], P('dp', 'rows'), may hold values from -40 to 40
- cotangent: bfloat16 [64, 48, 48, 768], P('dp', 'rows'), may hold values from -6 to 6
- dw_kernel: float32 [49, 768], replicated, may hold values from -0.875 to 0.875
- dw_bias: float32 [768], replicated, may hold values from -3 to 3
- ln_gain: float32 [768], replicated, may hold values from 0.5 to 1.5
- ln_bias: float32 [768], replicated, may hold values from -3 to 3
- w1: bfloat16 [768, 3072], P(None, 'dp'), may hold values from -0.21875 to 0.21875
- b1: bfloat16 [3072], P('dp'), may hold values from -3 to 3
- w2: bfloat16 [3072, 768], P('dp'), may hold values from -0.109375 to 0.109375
- b2: float32 [768], replicated, may hold values from -3 to 3
- gamma: float32 [768], replicated, may hold values from 0.3 to 1.5
Outputs:
- d_input: bfloat16 [64, 48, 48, 768], P('dp', 'rows')
- d_w1: float32 [768, 3072], P(None, 'dp')
- d_b1: float32 [3072], P('dp')
- d_w2: float32 [3072, 768], P('dp')
- param_grads: float32 [54, 768], replicated
The draws below stay inside these ranges and needn't reach their ends.
All inputs are finite; a program needn't handle non-finite values.
Results may differ from the reference program's by a relative error of at most 0.007.
Values may be sent and summed in bfloat16 or wider, within the bound.
No kernel may reach another device: no remote copies, remote signals or barrier semaphores. Data moves between devices by JAX's collectives and lax.ppermute only.
A program may use at most 128 MiB of HBM per device.

```python
import math
import jax
import jax.numpy as jnp
from jax import lax

C = 768
HID = 3072
COLS = 48
KERNEL = 7
TAPS = 49
BATCH = 64
HEIGHT = 48
PIXELS = 147456


def draw_block_input(key, part):
    key = jax.random.fold_in(key, 11)
    key_pixel, key_channel, key_core = jax.random.split(key, 3)
    shape = (BATCH, HEIGHT, COLS, C)
    pixel_scale = jnp.exp(jax.random.uniform(key_pixel, (BATCH, HEIGHT, COLS, 1), jnp.float32) * math.log(10.0))
    channel_scale = jnp.exp(jax.random.uniform(key_channel, (C,), jnp.float32) * math.log(10.0))
    core = jax.random.truncated_normal(key_core, -4.0, 4.0, shape, jnp.float32)
    return (core * pixel_scale * channel_scale * 0.1).astype(jnp.bfloat16)


def block_scale(rng, extent, shards, low, top_value):
    level, own = 1.0, jax.random.fold_in(rng, 6)
    for axis_at, blocks in shards:
        draws = jnp.exp(jax.random.uniform(jax.random.fold_in(own, axis_at), (blocks,), jnp.float32, low / len(shards), top_value / len(shards)))
        level = level * jnp.repeat(draws, extent[axis_at] // blocks).reshape([-1 if axis == axis_at else 1 for axis in range(len(extent))])
    return level


def scatter_about(key, shape, scale, most, pieces=(), dtype=jnp.bfloat16):
    entries = jax.random.normal(key, shape, jnp.float32) * scale
    if len(pieces) > 0:
        entries = block_scale(key, shape, pieces, -0.22, 0.18) * entries
    return jnp.clip(entries, min=-most, max=most).astype(dtype)


def setup_inputs(seed: int = 0) -> dict:
    streams_of = jax.random.split(jax.random.key(seed), 12)
    block_input = draw_block_input(jax.random.fold_in(streams_of[11], 71), 0)
    cotangent = scatter_about(streams_of[1], (BATCH, HEIGHT, COLS, C), 1.0, 6.0, ((0, 32), (1, 8)))
    dw_kernel = scatter_about(streams_of[2], (TAPS, C), TAPS ** -0.5, 0.875, (), jnp.float32)
    dw_bias = scatter_about(streams_of[3], (C,), 0.5, 3.0, (), jnp.float32)
    ln_gain = jnp.clip(jax.random.uniform(streams_of[4], (C,), jnp.float32, 0.5, 1.5), 0.5, 1.5)
    ln_bias = scatter_about(streams_of[5], (C,), 0.5, 3.0, (), jnp.float32)
    w1 = scatter_about(streams_of[6], (C, HID), C ** -0.5, 0.21875, ((1, 32),))
    b1 = scatter_about(streams_of[7], (HID,), 0.5, 3.0, ((0, 32),))
    w2 = scatter_about(streams_of[8], (HID, C), HID ** -0.5, 0.109375, ((0, 32),))
    b2 = scatter_about(streams_of[9], (C,), 0.5, 3.0, (), jnp.float32)
    gamma = jnp.clip(jnp.exp(jax.random.uniform(streams_of[10], (C,), jnp.float32, math.log(0.3), math.log(1.5))), 0.3, 1.5)
    return dict(block_input=block_input, cotangent=cotangent, dw_kernel=dw_kernel, dw_bias=dw_bias, ln_gain=ln_gain, ln_bias=ln_bias, w1=w1, b1=b1, w2=w2, b2=b2, gamma=gamma)


EPSILON = 1e-06
INV_ROOT_TWO = 0.7071067811865476
INV_ROOT_TWO_PI = 0.3989422804014327

def gelu_value(u):
    return 0.5 * u * (1.0 + lax.erf(u * INV_ROOT_TWO))

def gelu_slope(u):
    return 0.5 * (1.0 + lax.erf(u * INV_ROOT_TWO)) + u * jnp.exp(-0.5 * u * u) * INV_ROOT_TWO_PI

def depthwise(padded, kernel, height, width):
    total = jnp.zeros(padded.shape[:-3] + (height, width, padded.shape[-1]), jnp.float32)
    for row_tap in range(KERNEL):
        for col_tap in range(KERNEL):
            window = padded[..., row_tap:row_tap + height, col_tap:col_tap + width, :].astype(jnp.float32)
            total = total + window * kernel[row_tap * KERNEL + col_tap]
    return total

def transposed(padded_grad, kernel, height, width):
    reach = KERNEL - 1
    total = jnp.zeros(padded_grad.shape[:-3] + (height, width, padded_grad.shape[-1]), jnp.float32)
    for row_tap in range(KERNEL):
        for col_tap in range(KERNEL):
            window = padded_grad[..., reach - row_tap:reach - row_tap + height, reach - col_tap:reach - col_tap + width, :].astype(jnp.float32)
            total = total + window * kernel[row_tap * KERNEL + col_tap]
    return total

def tap_sums(padded, grad_conv, height, width):
    axes_all = tuple(range(grad_conv.ndim - 1))
    result_rows = []
    for row_tap in range(KERNEL):
        for col_tap in range(KERNEL):
            window = padded[..., row_tap:row_tap + height, col_tap:col_tap + width, :].astype(jnp.float32)
            result_rows.append(lax.optimization_barrier(jnp.sum(window * grad_conv, axis=axes_all)))
    return jnp.stack(result_rows)

def normalize(conv):
    center = conv - lax.optimization_barrier(jnp.mean(conv, axis=-1, keepdims=True))
    spread = lax.optimization_barrier(jnp.mean(center * center, axis=-1, keepdims=True))
    rstd = lax.rsqrt(spread + EPSILON)
    return (center * rstd, rstd)

def norm_backward(grad_normed, norm, rstd, ln_gain):
    weighted = grad_normed * ln_gain
    return rstd * (weighted - lax.optimization_barrier(jnp.mean(weighted, axis=-1, keepdims=True)) - norm * lax.optimization_barrier(jnp.mean(weighted * norm, axis=-1, keepdims=True)))

def reference(block_input, cotangent, dw_kernel, dw_bias, ln_gain, ln_bias, w1, b1, w2, b2, gamma):
    margin = KERNEL // 2
    chans = block_input.shape[-1]

    def one_image(carry, item):
        acc_w1, acc_moment, acc_b1, acc_small, acc_cot = carry
        image, cot_image = item
        padded = jnp.pad(image, ((margin, margin), (margin, margin), (0, 0)))
        conv = depthwise(padded, dw_kernel, HEIGHT, COLS) + dw_bias
        norm, rstd = normalize(conv)
        normed = (norm * ln_gain + ln_bias).astype(jnp.bfloat16).reshape(-1, chans)
        preact = jnp.dot(normed, w1, preferred_element_type=jnp.float32) + b1.astype(jnp.float32)
        hidden = gelu_value(preact).astype(jnp.bfloat16)
        flat_cot = cot_image.reshape(-1, chans).astype(jnp.float32)
        scaled = (flat_cot * gamma).astype(jnp.bfloat16)
        grad_hidden = lax.dot_general(scaled, w2, (((1,), (1,)), ((), ())), preferred_element_type=jnp.float32)
        grad_preact = (grad_hidden * gelu_slope(preact)).astype(jnp.bfloat16)
        grad_normed = lax.dot_general(grad_preact, w1, (((1,), (1,)), ((), ())), preferred_element_type=jnp.float32).reshape(conv.shape)
        grad_conv = norm_backward(grad_normed, norm, rstd, ln_gain).astype(jnp.bfloat16)
        grad_wide = grad_conv.astype(jnp.float32)
        padded_grad = jnp.pad(grad_conv, ((margin, margin), (margin, margin), (0, 0)))
        d_image = (cot_image.astype(jnp.float32) + transposed(padded_grad, dw_kernel, HEIGHT, COLS)).astype(jnp.bfloat16)
        moment = lax.dot_general(hidden, scaled, (((0,), (0,)), ((), ())), preferred_element_type=jnp.float32)
        term_w1 = lax.dot_general(normed, grad_preact, (((0,), (0,)), ((), ())), preferred_element_type=jnp.float32)
        term_b1 = lax.optimization_barrier(jnp.sum(grad_preact.astype(jnp.float32), axis=0))
        small = jnp.concatenate([tap_sums(padded, grad_wide, HEIGHT, COLS), lax.optimization_barrier(jnp.sum(grad_wide, axis=(0, 1)))[None], lax.optimization_barrier(jnp.sum(grad_normed * norm, axis=(0, 1)))[None], lax.optimization_barrier(jnp.sum(grad_normed, axis=(0, 1)))[None]], axis=0)
        carry = (acc_w1 + term_w1, acc_moment + moment, acc_b1 + term_b1, acc_small + small, acc_cot + lax.optimization_barrier(jnp.sum(flat_cot, axis=0)))
        return (carry, d_image)
    init = (jnp.zeros((chans, HID), jnp.float32), jnp.zeros((HID, chans), jnp.float32), jnp.zeros((HID,), jnp.float32), jnp.zeros((TAPS + 3, chans), jnp.float32), jnp.zeros((chans,), jnp.float32))
    totals, d_input = lax.scan(one_image, init, (block_input, cotangent))
    total_w1, moment, total_b1, small, cot_sums = totals
    factor = 1.0 / PIXELS ** 0.5
    layer_rows = jnp.stack([gamma * cot_sums, lax.optimization_barrier(jnp.sum(w2.astype(jnp.float32) * moment, axis=0)) / gamma + b2 * cot_sums])
    param_grads = jnp.concatenate([small, layer_rows], axis=0) * factor
    return (d_input, total_w1 * factor, total_b1 * factor, moment * factor, param_grads)
```

```python
import math

import jax
import jax.numpy as jnp
import numpy as np
from jax import lax
from jax.sharding import Mesh, PartitionSpec as P

KERNEL = 7
MARGIN = 3
EPSILON = 1e-06
INV_ROOT_TWO = 0.7071067811865476
INV_ROOT_TWO_PI = 0.3989422804014327

AXES = ("y_lo", "z", "core", "y_hi", "x")
SIZES = (2, 8, 2, 2, 4)
DP = ("y_lo", "z", "core")
ROWS = ("y_hi", "x")
PAIRS = ("y_lo", "z")


def halo(cells):
    down = [(i, i + 1) for i in range(7)]
    up = [(i + 1, i) for i in range(7)]
    above = lax.ppermute(cells[:, -MARGIN:], ROWS, down)
    below = lax.ppermute(cells[:, :MARGIN], ROWS, up)
    return jnp.concatenate([above, cells, below], axis=1)


def swap(cells):
    return lax.ppermute(cells, "core", [(0, 1), (1, 0)])


def spread_sum(part, axes):
    count = lax.axis_size(axes)
    pieces = part.reshape((count, part.shape[0] // count) + part.shape[1:])
    pieces = lax.all_to_all(pieces, axes, 0, 0)
    return jnp.sum(pieces.astype(jnp.float32), axis=0)


def gather(part, axes):
    count = lax.axis_size(axes)
    return lax.all_to_all(jnp.broadcast_to(part[None], (count,) + part.shape), axes, 0, 0)


def total(small):
    size = small.size
    flat = jnp.pad(small.reshape(-1), (0, -size % (16 * 1024))).reshape(16, -1, 128)
    part = spread_sum(flat, ("core",) + ROWS)
    part = jnp.sum(gather(part, PAIRS), axis=0)
    return gather(part, ("core",) + ROWS).reshape(-1)[:size].reshape(small.shape)


def pad_columns(cells):
    return jnp.pad(cells, ((0, 0), (0, 0), (MARGIN, MARGIN), (0, 0)))


def depthwise(padded, kernel, height, width):
    total = jnp.zeros(padded.shape[:-3] + (height, width, padded.shape[-1]), jnp.float32)
    for row_tap in range(KERNEL):
        for col_tap in range(KERNEL):
            window = padded[:, row_tap : row_tap + height, col_tap : col_tap + width]
            total = total + window.astype(jnp.float32) * kernel[row_tap * KERNEL + col_tap]
    return total


def tap_sums(padded, grad_conv, height, width):
    rows = []
    for row_tap in range(KERNEL):
        for col_tap in range(KERNEL):
            window = padded[:, row_tap : row_tap + height, col_tap : col_tap + width]
            rows.append(jnp.sum(window.astype(jnp.float32) * grad_conv, axis=(0, 1, 2)))
    return jnp.stack(rows)


def shards(block_input, cotangent, dw_kernel, dw_bias, ln_gain, ln_bias, w1, b1, w2, b2, gamma):
    images, rows_here, cols, chans = block_input.shape
    shard = w1.shape[1]
    pixels = images * rows_here * cols
    flat_cot = cotangent.reshape(pixels, chans).astype(jnp.float32)
    scaled = (flat_cot * gamma).astype(jnp.bfloat16)
    packed = jnp.concatenate(
        [w1.T, w2, jnp.broadcast_to(b1[:, None], (shard, 128))], axis=1
    )
    weights = lax.all_gather(packed, PAIRS, axis=0, tiled=True)
    w1_t, w2_h = weights[:, :chans], weights[:, chans : 2 * chans]
    b1_h = weights[:, 2 * chans].astype(jnp.float32)

    padded = pad_columns(halo(block_input))
    scaled2 = jnp.concatenate([scaled, swap(scaled)], axis=0)
    conv = depthwise(padded, dw_kernel, rows_here, cols) + dw_bias
    center = conv - jnp.mean(conv, axis=-1, keepdims=True)
    spread = jnp.mean(center * center, axis=-1, keepdims=True)
    rstd = lax.rsqrt(spread + EPSILON).reshape(pixels, 1)
    norm = center.reshape(pixels, chans) * rstd
    normed = (norm * ln_gain + ln_bias).astype(jnp.bfloat16)
    normed2 = jnp.concatenate([normed, swap(normed)], axis=0)

    nt = (((1,), (1,)), ((), ()))
    nn = (((1,), (0,)), ((), ()))
    tn = (((0,), (0,)), ((), ()))
    preact = lax.dot_general(normed2, w1_t, nt, preferred_element_type=jnp.float32) + b1_h
    grad_hidden = lax.dot_general(scaled2, w2_h, nt, preferred_element_type=jnp.float32)
    cdf = 0.5 * (1.0 + lax.erf(preact * INV_ROOT_TWO))
    hidden = (preact * cdf).astype(jnp.bfloat16)
    slope = cdf + preact * jnp.exp(-0.5 * preact * preact) * INV_ROOT_TWO_PI
    grad_preact = (grad_hidden * slope).astype(jnp.bfloat16)

    grad_normed2 = lax.dot_general(grad_preact, w1_t, nn, preferred_element_type=jnp.float32)
    grad_normed = grad_normed2[:pixels] + swap(grad_normed2[pixels:].astype(jnp.bfloat16)).astype(
        jnp.float32
    )
    moment = lax.dot_general(hidden, scaled2, tn, preferred_element_type=jnp.float32)
    term_w1 = lax.dot_general(grad_preact, normed2, tn, preferred_element_type=jnp.float32)
    terms = jnp.concatenate([term_w1, moment], axis=1).astype(jnp.bfloat16)
    share = lax.psum_scatter(terms, PAIRS, scatter_dimension=0, tiled=True)
    share = gather(spread_sum(share, ROWS).astype(jnp.bfloat16), ROWS)
    share = share.reshape(shard, 2 * chans).astype(jnp.float32)

    weighted = grad_normed * ln_gain
    grad_conv = (
        rstd
        * (
            weighted
            - jnp.mean(weighted, axis=-1, keepdims=True)
            - norm * jnp.mean(weighted * norm, axis=-1, keepdims=True)
        )
    ).astype(jnp.bfloat16)
    grad_maps = grad_conv.reshape(block_input.shape)
    grad_padded = pad_columns(halo(grad_maps))
    d_input = (
        cotangent.astype(jnp.float32)
        + depthwise(grad_padded, dw_kernel[::-1], rows_here, cols)
    ).astype(jnp.bfloat16)

    grad_wide = grad_maps.astype(jnp.float32)
    cot_sums = jnp.sum(flat_cot, axis=0)
    core = lax.axis_index("core")
    hid = b1_h.shape[0]
    sums_b1 = jnp.sum(grad_preact.astype(jnp.float32), axis=0)
    pair_b1 = jnp.where(core == jnp.arange(2)[:, None], sums_b1[None], 0.0)
    local_small = jnp.concatenate(
        [
            tap_sums(padded, grad_wide, rows_here, cols),
            jnp.sum(grad_wide, axis=(0, 1, 2))[None],
            jnp.sum(grad_normed * norm, axis=0)[None],
            jnp.sum(grad_normed, axis=0)[None],
            (gamma * cot_sums)[None],
            (jnp.sum(w2_h.astype(jnp.float32) * moment, axis=0) / gamma + b2 * cot_sums)[None],
            pair_b1.reshape(-1, chans),
        ],
        axis=0,
    )
    total_small = total(local_small)
    factor = 1.0 / math.sqrt(pixels * 256)
    param_grads = total_small[:54] * factor
    at = (lax.axis_index("y_lo") * 8 + lax.axis_index("z")) * shard
    d_b1 = lax.dynamic_slice(
        total_small[54:].reshape(2, hid), (core, at), (1, shard)
    ).reshape(shard) * factor
    share = share * factor
    d_w1, d_w2 = share[:, :chans].T, share[:, chans:]
    return (d_input.reshape(block_input.shape), d_w1, d_b1, d_w2, param_grads)


def solution(mesh):
    fine = Mesh(mesh.devices.reshape(SIZES), AXES)
    placed = (
        P(DP, ROWS, None, None),
        P(DP, ROWS, None, None),
        P(),
        P(),
        P(),
        P(),
        P(None, DP),
        P(DP),
        P(DP, None),
        P(),
        P(),
    )
    return jax.shard_map(
        shards,
        mesh=fine,
        in_specs=placed,
        out_specs=(P(DP, ROWS, None, None), P(None, DP), P(DP), P(DP, None), P()),
        check_vma=False,
    )
```

```python
import math

import jax
import jax.numpy as jnp
import numpy as np
from jax import lax
from jax.sharding import Mesh, PartitionSpec as P

KERNEL = 7
MARGIN = 3
EPSILON = 1e-06
INV_ROOT_TWO = 0.7071067811865476
INV_ROOT_TWO_PI = 0.3989422804014327

AXES = ("y_lo", "z", "core", "y_hi", "x")
SIZES = (2, 8, 2, 2, 4)
DP = ("y_lo", "z", "core")
ROWS = ("y_hi", "x")
PAIRS = ("y_lo", "z")
Y = ("y_lo", "y_hi")


def halo(cells):
    down = [(i, i + 1) for i in range(7)]
    up = [(i + 1, i) for i in range(7)]
    above = lax.ppermute(cells[:, -MARGIN:], ROWS, down)
    below = lax.ppermute(cells[:, :MARGIN], ROWS, up)
    return jnp.concatenate([above, cells, below], axis=1)


def swap(cells):
    return lax.ppermute(cells, "core", [(0, 1), (1, 0)])


def spread_sum(part, axes):
    count = lax.axis_size(axes)
    pieces = part.reshape((count, part.shape[0] // count) + part.shape[1:])
    pieces = lax.all_to_all(pieces, axes, 0, 0)
    return jnp.sum(pieces.astype(jnp.float32), axis=0)


def gather(part, axes):
    count = lax.axis_size(axes)
    return lax.all_to_all(jnp.broadcast_to(part[None], (count,) + part.shape), axes, 0, 0)


def total(small):
    size = small.size
    flat = jnp.pad(small.reshape(-1), (0, -size % (16 * 1024))).reshape(16, -1, 128)
    part = spread_sum(flat, ("core",) + ROWS)
    part = jnp.sum(gather(part, PAIRS), axis=0)
    return gather(part, ("core",) + ROWS).reshape(-1)[:size].reshape(small.shape)


def gather_weights(w1_t, w2):
    x, y_hi = lax.axis_index("x"), lax.axis_index("y_hi")
    at = ((x % 2) * 48 + y_hi * 24, (x // 2) * 384)
    mine = jnp.stack([lax.dynamic_slice(w, at, (24, 384)) for w in (w1_t, w2)])
    first, second = jnp.moveaxis(gather(mine, "z"), 1, 0)
    first = gather(gather(first, Y), "x").reshape(2, 2, 4, 8 * 24, 384)
    second = gather(gather(second, "x"), Y).reshape(4, 2, 2, 8 * 24, 384)
    return (
        first.transpose(1, 2, 3, 0, 4).reshape(-1, 768),
        second.transpose(2, 0, 3, 1, 4).reshape(-1, 768),
    )


def scatter_terms(term_w1, moment):
    first = term_w1.astype(jnp.bfloat16).reshape(2, 4, 192, 2, 384).transpose(3, 0, 1, 2, 4)
    second = moment.astype(jnp.bfloat16).reshape(2, 4, 192, 2, 384).transpose(1, 3, 0, 2, 4)
    second = spread_sum(second.reshape(-1, 384), Y).astype(jnp.bfloat16)
    first = spread_sum(first.reshape(-1, 384), "x").astype(jnp.bfloat16)
    second = spread_sum(second, "x").astype(jnp.bfloat16)
    first = spread_sum(first, Y).astype(jnp.bfloat16)
    both = spread_sum(jnp.concatenate([first, second], axis=1), "z").astype(jnp.bfloat16)
    blocks = gather(both, ROWS).reshape(2, 2, 2, 24, 2, 384).astype(jnp.float32)
    blocks = blocks.transpose(4, 2, 0, 3, 1, 5).reshape(2, 96, 768)
    return blocks[0], blocks[1]


def pad_columns(cells):
    return jnp.pad(cells, ((0, 0), (0, 0), (MARGIN, MARGIN), (0, 0)))


def depthwise(padded, kernel, height, width):
    total = jnp.zeros(padded.shape[:-3] + (height, width, padded.shape[-1]), jnp.float32)
    for row_tap in range(KERNEL):
        for col_tap in range(KERNEL):
            window = padded[:, row_tap : row_tap + height, col_tap : col_tap + width]
            total = total + window.astype(jnp.float32) * kernel[row_tap * KERNEL + col_tap]
    return total


def tap_sums(padded, grad_conv, height, width):
    rows = []
    for row_tap in range(KERNEL):
        for col_tap in range(KERNEL):
            window = padded[:, row_tap : row_tap + height, col_tap : col_tap + width]
            rows.append(jnp.sum(window.astype(jnp.float32) * grad_conv, axis=(0, 1, 2)))
    return jnp.stack(rows)


def shards(block_input, cotangent, dw_kernel, dw_bias, ln_gain, ln_bias, w1, b1, w2, b2, gamma):
    images, rows_here, cols, chans = block_input.shape
    shard = w1.shape[1]
    pixels = images * rows_here * cols
    flat_cot = cotangent.reshape(pixels, chans).astype(jnp.float32)
    scaled = (flat_cot * gamma).astype(jnp.bfloat16)
    w1_t, w2_h = gather_weights(w1.T, w2)
    b1_h = gather(b1.astype(jnp.float32), PAIRS).reshape(2, 8, 2, 2, 24)
    b1_h = b1_h.transpose(2, 0, 3, 1, 4).reshape(-1)

    padded = pad_columns(halo(block_input))
    scaled2 = jnp.concatenate([scaled, swap(scaled)], axis=0)
    conv = depthwise(padded, dw_kernel, rows_here, cols) + dw_bias
    center = conv - jnp.mean(conv, axis=-1, keepdims=True)
    spread = jnp.mean(center * center, axis=-1, keepdims=True)
    rstd = lax.rsqrt(spread + EPSILON).reshape(pixels, 1)
    norm = center.reshape(pixels, chans) * rstd
    normed = (norm * ln_gain + ln_bias).astype(jnp.bfloat16)
    normed2 = jnp.concatenate([normed, swap(normed)], axis=0)

    nt = (((1,), (1,)), ((), ()))
    nn = (((1,), (0,)), ((), ()))
    tn = (((0,), (0,)), ((), ()))
    preact = lax.dot_general(normed2, w1_t, nt, preferred_element_type=jnp.float32) + b1_h
    grad_hidden = lax.dot_general(scaled2, w2_h, nt, preferred_element_type=jnp.float32)
    cdf = 0.5 * (1.0 + lax.erf(preact * INV_ROOT_TWO))
    hidden = (preact * cdf).astype(jnp.bfloat16)
    slope = cdf + preact * jnp.exp(-0.5 * preact * preact) * INV_ROOT_TWO_PI
    grad_preact = (grad_hidden * slope).astype(jnp.bfloat16)

    grad_normed2 = lax.dot_general(grad_preact, w1_t, nn, preferred_element_type=jnp.float32)
    grad_normed = grad_normed2[:pixels] + swap(grad_normed2[pixels:].astype(jnp.bfloat16)).astype(
        jnp.float32
    )
    moment = lax.dot_general(hidden, scaled2, tn, preferred_element_type=jnp.float32)
    term_w1 = lax.dot_general(grad_preact, normed2, tn, preferred_element_type=jnp.float32)
    d_w1, d_w2 = scatter_terms(term_w1, moment)

    weighted = grad_normed * ln_gain
    grad_conv = (
        rstd
        * (
            weighted
            - jnp.mean(weighted, axis=-1, keepdims=True)
            - norm * jnp.mean(weighted * norm, axis=-1, keepdims=True)
        )
    ).astype(jnp.bfloat16)
    grad_maps = grad_conv.reshape(block_input.shape)
    grad_padded = pad_columns(halo(grad_maps))
    d_input = (
        cotangent.astype(jnp.float32)
        + depthwise(grad_padded, dw_kernel[::-1], rows_here, cols)
    ).astype(jnp.bfloat16)

    grad_wide = grad_maps.astype(jnp.float32)
    cot_sums = jnp.sum(flat_cot, axis=0)
    core = lax.axis_index("core")
    hid = b1_h.shape[0]
    sums_b1 = jnp.sum(grad_preact.astype(jnp.float32), axis=0)
    pair_b1 = jnp.where(core == jnp.arange(2)[:, None], sums_b1[None], 0.0)
    local_small = jnp.concatenate(
        [
            tap_sums(padded, grad_wide, rows_here, cols),
            jnp.sum(grad_wide, axis=(0, 1, 2))[None],
            jnp.sum(grad_normed * norm, axis=0)[None],
            jnp.sum(grad_normed, axis=0)[None],
            (gamma * cot_sums)[None],
            (jnp.sum(w2_h.astype(jnp.float32) * moment, axis=0) / gamma + b2 * cot_sums)[None],
            pair_b1.reshape(-1, chans),
        ],
        axis=0,
    )
    total_small = total(local_small)
    factor = 1.0 / math.sqrt(pixels * 256)
    param_grads = total_small[:54] * factor
    sums = total_small[54:].reshape(2, 2, 2, 2, 8, 24)
    mine = (core, 0, lax.axis_index("y_lo"), 0, lax.axis_index("z"), 0)
    d_b1 = lax.dynamic_slice(sums, mine, (1, 2, 1, 2, 1, 24)).reshape(shard) * factor
    d_w1, d_w2 = (d_w1 * factor).T, d_w2 * factor
    return (d_input.reshape(block_input.shape), d_w1, d_b1, d_w2, param_grads)


def solution(mesh):
    fine = Mesh(mesh.devices.reshape(SIZES), AXES)
    placed = (
        P(DP, ROWS, None, None),
        P(DP, ROWS, None, None),
        P(),
        P(),
        P(),
        P(),
        P(None, DP),
        P(DP),
        P(DP, None),
        P(),
        P(),
    )
    return jax.shard_map(
        shards,
        mesh=fine,
        in_specs=placed,
        out_specs=(P(DP, ROWS, None, None), P(None, DP), P(DP), P(DP, None), P()),
        check_vma=False,
    )
```

```python
import math

import jax
import jax.numpy as jnp
import numpy as np
from jax import lax
from jax.experimental import pallas as pl
from jax.experimental.pallas import tpu as pltpu
from jax.sharding import Mesh, PartitionSpec as P

KERNEL = 7
MARGIN = 3
EPSILON = 1e-06
INV_ROOT_TWO = 0.7071067811865476
INV_ROOT_TWO_PI = 0.3989422804014327

AXES = ("y_lo", "z", "core", "y_hi", "x")
SIZES = (2, 8, 2, 2, 4)
DP = ("y_lo", "z", "core")
ROWS = ("y_hi", "x")
PAIRS = ("y_lo", "z")
Y = ("y_lo", "y_hi")


def halo(cells):
    down = [(i, i + 1) for i in range(7)]
    up = [(i + 1, i) for i in range(7)]
    above = lax.ppermute(cells[:, -MARGIN:], ROWS, down)
    below = lax.ppermute(cells[:, :MARGIN], ROWS, up)
    return jnp.concatenate([above, cells, below], axis=1)


def swap(cells):
    return lax.ppermute(cells, "core", [(0, 1), (1, 0)])


def spread_sum(part, axes):
    count = lax.axis_size(axes)
    pieces = part.reshape((count, part.shape[0] // count) + part.shape[1:])
    pieces = lax.all_to_all(pieces, axes, 0, 0)
    return jnp.sum(pieces.astype(jnp.float32), axis=0)


def gather(part, axes):
    count = lax.axis_size(axes)
    return lax.all_to_all(jnp.broadcast_to(part[None], (count,) + part.shape), axes, 0, 0)


def total(small):
    size = small.size
    flat = jnp.pad(small.reshape(-1), (0, -size % (16 * 1024))).reshape(16, -1, 128)
    part = spread_sum(flat, ("core",) + ROWS)
    part = jnp.sum(gather(part, PAIRS), axis=0)
    return gather(part, ("core",) + ROWS).reshape(-1)[:size].reshape(small.shape)


def shift(cells, ring, step):
    if ring == "x":
        return lax.ppermute(cells, "x", [(i, (i + step) % 4) for i in range(4)])
    place = [(y % 2) * 2 + y // 2 for y in range(4)]
    return lax.ppermute(cells, Y, [(place[y], place[(y + step) % 4]) for y in range(4)])


def ring_gather(mine, ring):
    half = mine.shape[0] // 2
    left = shift(mine, ring, 1)
    right = shift(mine, ring, -1)
    far = [shift(left[:half], ring, 1), shift(right[half:], ring, -1)]
    return [mine, right, jnp.concatenate(far, axis=0), left]


def ring_sum(parts, ring):
    half = parts[2].shape[0] // 2
    wide = [part.astype(jnp.float32) for part in parts]
    up = shift(parts[2][:half], ring, 1).astype(jnp.float32)
    down = shift(parts[2][half:], ring, -1).astype(jnp.float32)
    right = jnp.concatenate([wide[1][:half] + up, wide[1][half:]], axis=0)
    left = jnp.concatenate([wide[3][:half], wide[3][half:] + down], axis=0)
    right = shift(right.astype(jnp.bfloat16), ring, 1)
    left = shift(left.astype(jnp.bfloat16), ring, -1)
    return wide[0] + right.astype(jnp.float32) + left.astype(jnp.float32)


def y_flags():
    y = lax.axis_index("y_hi") * 2 + lax.axis_index("y_lo")
    return y // 2 == 1, ((y + 1) % 4) // 2 == 1


def join(one, other, second):
    return jnp.where(
        second,
        jnp.concatenate([other, one], axis=1),
        jnp.concatenate([one, other], axis=1),
    )


def cut(cells, second):
    low, high = cells[:, :384], cells[:, 384:]
    return jnp.where(second, high, low), jnp.where(second, low, high)


def gather_weights(w1_t, w2, b1):
    x, y_hi = lax.axis_index("x"), lax.axis_index("y_hi")
    mine = [lax.dynamic_slice(w, (x * 24, y_hi * 384), (24, 384)) for w in (w1_t, w2)]
    bias = jnp.pad(b1[None], ((0, 7), (0, 384 - b1.shape[0])))
    along_z = gather(jnp.concatenate(mine + [bias], axis=0), "z")
    first = along_z[:, :24].reshape(192, 384)
    second = along_z[:, 24:48].reshape(192, 384)
    here, there = y_flags()
    first = ring_gather(first, "y")
    second = jnp.concatenate(ring_gather(second, "x"), axis=0)
    first = jnp.concatenate(
        [join(first[0], first[2], here), join(first[1], first[3], there)], axis=0
    )
    second = ring_gather(second, "y")
    first = jnp.concatenate(ring_gather(first, "x"), axis=0)
    second = jnp.stack(
        [
            join(second[0], second[2], here).reshape(4, 192, 768),
            join(second[1], second[3], there).reshape(4, 192, 768),
        ],
        axis=1,
    ).reshape(-1, 768)
    bias = along_z[:, 48, :96]
    bias = jnp.stack([bias, shift(bias, "y", 1)]).reshape(2, 8, 4, 24).astype(jnp.float32)
    bias = jnp.roll(bias, -x, axis=2).transpose(2, 0, 1, 3).reshape(-1)
    return first, second, bias


def scatter_terms(term_w1, moment):
    here, there = y_flags()
    moment = moment.reshape(4, 2, 192, 768)
    near = cut(moment[:, 0].reshape(768, 768), here)
    next_to = cut(moment[:, 1].reshape(768, 768), there)
    second = ring_sum([near[0], next_to[0], near[1], next_to[1]], "y")
    first = ring_sum([term_w1[k * 384 : (k + 1) * 384] for k in range(4)], "x")
    second = second.astype(jnp.bfloat16)
    first = first.astype(jnp.bfloat16)
    near, next_to = cut(first[:192], here), cut(first[192:], there)
    first = ring_sum([near[0], next_to[0], near[1], next_to[1]], "y")
    second = ring_sum([second[k * 192 : (k + 1) * 192] for k in range(4)], "x")
    both = jnp.concatenate([first, second], axis=1).astype(jnp.bfloat16)
    both = spread_sum(both, "z").astype(jnp.bfloat16)
    blocks = gather(both, ROWS).reshape(2, 4, 24, 2, 384).astype(jnp.float32)
    blocks = blocks.transpose(3, 1, 2, 0, 4).reshape(2, 96, 768)
    return blocks[0], blocks[1]


BLOCK = 256
LANES = 128
NT = (((1,), (1,)), ((), ()))
NN = (((1,), (0,)), ((), ()))
TN = (((0,), (0,)), ((), ()))
VMEM = 50 * 2**20


def mlp_kernel(normed, scaled, w1, w2, b1, d_w1, moment, grad_normed, d_b1, row):
    @pl.when(pl.program_id(0) == 0)
    def _():
        grad_normed[...] = jnp.zeros_like(grad_normed)
        row[...] = jnp.zeros_like(row)

    n, s = normed[...], scaled[...]
    preact = lax.dot_general(w1[...], n, NT, preferred_element_type=jnp.float32) + b1[:, :1]
    cdf = 0.5 * (1.0 + lax.erf(preact * INV_ROOT_TWO))
    hidden = (preact * cdf).astype(jnp.bfloat16)
    slope = cdf + preact * jnp.exp(-0.5 * preact * preact) * INV_ROOT_TWO_PI
    grad_hidden = lax.dot_general(w2[...], s, NT, preferred_element_type=jnp.float32)
    grad_preact = (grad_hidden * slope).astype(jnp.bfloat16)
    total = lax.dot_general(hidden, s, NN, preferred_element_type=jnp.float32)
    moment[...] = total.astype(jnp.bfloat16)
    row[...] += jnp.sum(total * w2[...].astype(jnp.float32), axis=0, keepdims=True)
    d_w1[...] = lax.dot_general(grad_preact, n, NN, preferred_element_type=jnp.float32).astype(
        jnp.bfloat16
    )
    d_b1[...] = jnp.broadcast_to(
        jnp.sum(grad_preact.astype(jnp.float32), axis=1, keepdims=True), d_b1.shape
    )
    grad_normed[...] += lax.dot_general(
        grad_preact, w1[...], TN, preferred_element_type=jnp.float32
    )


def mlp(normed, scaled, w1, w2, b1):
    pixels, chans = normed.shape
    hid = w1.shape[0]
    whole = pl.BlockSpec((pixels, chans), lambda i: (0, 0))
    block = pl.BlockSpec((BLOCK, chans), lambda i: (i, 0))
    lane = pl.BlockSpec((BLOCK, LANES), lambda i: (i, 0))
    return pl.pallas_call(
        mlp_kernel,
        grid=(hid // BLOCK,),
        in_specs=[whole, whole, block, block, lane],
        out_specs=[block, block, whole, lane, pl.BlockSpec((1, chans), lambda i: (0, 0))],
        out_shape=[
            jax.ShapeDtypeStruct((hid, chans), jnp.bfloat16),
            jax.ShapeDtypeStruct((hid, chans), jnp.bfloat16),
            jax.ShapeDtypeStruct((pixels, chans), jnp.float32),
            jax.ShapeDtypeStruct((hid, LANES), jnp.float32),
            jax.ShapeDtypeStruct((1, chans), jnp.float32),
        ],
        compiler_params=pltpu.CompilerParams(vmem_limit_bytes=VMEM),
        cost_estimate=pl.CostEstimate(
            flops=10 * pixels * hid * chans, bytes_accessed=2**24, transcendentals=2 * pixels * hid
        ),
    )(normed, scaled, w1, w2, jnp.broadcast_to(b1[:, None], (hid, LANES)))


def transposed_kernel(padded, cotangent, kernel, d_input, wide):
    rows, cols = d_input.shape[1:3]
    wide[...] = padded[0].astype(jnp.float32)
    for at in range(0, cols, 24):
        sums = [cotangent[0, r, at : at + 24].astype(jnp.float32) for r in range(rows)]
        for b in range(KERNEL):
            column = [(KERNEL - 1 - a) * KERNEL + KERNEL - 1 - b for a in range(KERNEL)]
            taps = [kernel[t : t + 1] for t in column]
            for r in range(rows + KERNEL - 1):
                cells = wide[r, at + b : at + b + 24]
                for a in range(max(0, r - rows + 1), min(KERNEL, r + 1)):
                    sums[r - a] = sums[r - a] + cells * taps[a]
        for r in range(rows):
            d_input[0, r, at : at + 24] = sums[r].astype(jnp.bfloat16)


def transposed(padded, cotangent, kernel):
    images, high, wide, chans = padded.shape
    rows, cols = cotangent.shape[1:3]
    maps = pl.BlockSpec((1, rows, cols, LANES), lambda c, i: (i, 0, 0, c))
    return pl.pallas_call(
        transposed_kernel,
        grid=(chans // LANES, images),
        in_specs=[
            pl.BlockSpec((1, high, wide, LANES), lambda c, i: (i, 0, 0, c)),
            maps,
            pl.BlockSpec((KERNEL * KERNEL, LANES), lambda c, i: (0, c)),
        ],
        out_specs=maps,
        out_shape=jax.ShapeDtypeStruct(cotangent.shape, jnp.bfloat16),
        scratch_shapes=[pltpu.VMEM((high, wide, LANES), jnp.float32)],
        compiler_params=pltpu.CompilerParams(vmem_limit_bytes=VMEM),
        cost_estimate=pl.CostEstimate(
            flops=10**10, bytes_accessed=2**22, transcendentals=0
        ),
    )(padded, cotangent, kernel)


def taps_kernel(padded, grad, sums, wide, grad_wide):
    rows, cols = grad.shape[1:3]
    wide[...] = padded[0].astype(jnp.float32)
    grad_wide[...] = grad[0].astype(jnp.float32)

    @pl.when(pl.program_id(1) == 0)
    def _():
        sums[...] = jnp.zeros_like(sums)

    for b in range(KERNEL):
        totals = [jnp.zeros((8, LANES), jnp.float32) for _ in range(KERNEL)]
        for at in range(0, cols, 16):
            own = [grad_wide[r, at : at + 16] for r in range(rows)]
            for r in range(rows + KERNEL - 1):
                cells = wide[r, at + b : at + b + 16]
                for a in range(max(0, r - rows + 1), min(KERNEL, r + 1)):
                    product = cells * own[r - a]
                    totals[a] = totals[a] + (product[:8] + product[8:])
        for a in range(KERNEL):
            t = a * KERNEL + b
            sums[t : t + 1] += jnp.sum(totals[a], axis=0, keepdims=True)


def tap_sums(padded, grad):
    images, high, wide, chans = padded.shape
    rows, cols = grad.shape[1:3]
    return pl.pallas_call(
        taps_kernel,
        grid=(chans // LANES, images),
        in_specs=[
            pl.BlockSpec((1, high, wide, LANES), lambda c, i: (i, 0, 0, c)),
            pl.BlockSpec((1, rows, cols, LANES), lambda c, i: (i, 0, 0, c)),
        ],
        out_specs=pl.BlockSpec((KERNEL * KERNEL, LANES), lambda c, i: (0, c)),
        out_shape=jax.ShapeDtypeStruct((KERNEL * KERNEL, chans), jnp.float32),
        scratch_shapes=[
            pltpu.VMEM((high, wide, LANES), jnp.float32),
            pltpu.VMEM((rows, cols, LANES), jnp.float32),
        ],
        compiler_params=pltpu.CompilerParams(vmem_limit_bytes=VMEM),
        cost_estimate=pl.CostEstimate(
            flops=10**10, bytes_accessed=2**22, transcendentals=0
        ),
    )(padded, grad)


def pad_columns(cells):
    return jnp.pad(cells, ((0, 0), (0, 0), (MARGIN, 8 - MARGIN), (0, 0)))


def depthwise(padded, kernel, height, width):
    total = jnp.zeros(padded.shape[:-3] + (height, width, padded.shape[-1]), jnp.float32)
    for row_tap in range(KERNEL):
        for col_tap in range(KERNEL):
            window = padded[:, row_tap : row_tap + height, col_tap : col_tap + width]
            total = total + window.astype(jnp.float32) * kernel[row_tap * KERNEL + col_tap]
    return total


def shards(block_input, cotangent, dw_kernel, dw_bias, ln_gain, ln_bias, w1, b1, w2, b2, gamma):
    images, rows_here, cols, chans = block_input.shape
    shard = w1.shape[1]
    pixels = images * rows_here * cols
    flat_cot = cotangent.reshape(pixels, chans).astype(jnp.float32)
    scaled = (flat_cot * gamma).astype(jnp.bfloat16)
    w1_t, w2_h, b1_h = gather_weights(w1.T, w2, b1)

    padded = pad_columns(halo(block_input))
    scaled2 = jnp.concatenate([scaled, swap(scaled)], axis=0)
    conv = depthwise(padded, dw_kernel, rows_here, cols) + dw_bias
    center = conv - jnp.mean(conv, axis=-1, keepdims=True)
    spread = jnp.mean(center * center, axis=-1, keepdims=True)
    rstd = lax.rsqrt(spread + EPSILON).reshape(pixels, 1)
    norm = center.reshape(pixels, chans) * rstd
    normed = (norm * ln_gain + ln_bias).astype(jnp.bfloat16)
    normed2 = jnp.concatenate([normed, swap(normed)], axis=0)

    term_w1, moment, grad_normed2, sums_b1, moment_row = mlp(normed2, scaled2, w1_t, w2_h, b1_h)
    grad_normed = grad_normed2[:pixels] + swap(grad_normed2[pixels:].astype(jnp.bfloat16)).astype(
        jnp.float32
    )
    d_w1, d_w2 = scatter_terms(term_w1, moment)

    weighted = grad_normed * ln_gain
    grad_conv = (
        rstd
        * (
            weighted
            - jnp.mean(weighted, axis=-1, keepdims=True)
            - norm * jnp.mean(weighted * norm, axis=-1, keepdims=True)
        )
    ).astype(jnp.bfloat16)
    grad_maps = grad_conv.reshape(block_input.shape)
    grad_padded = pad_columns(halo(grad_maps))
    d_input = transposed(grad_padded, cotangent, dw_kernel)

    grad_wide = grad_maps.astype(jnp.float32)
    cot_sums = jnp.sum(flat_cot, axis=0)
    core = lax.axis_index("core")
    x, y_lo = lax.axis_index("x"), lax.axis_index("y_lo")
    sums_b1 = jnp.roll(sums_b1[:, 0].reshape(4, 2, 8, 24), (x, y_lo), (0, 1)).reshape(1, -1)
    pair_b1 = jnp.where(core == jnp.arange(2)[:, None], sums_b1, 0.0)
    local_small = jnp.concatenate(
        [
            tap_sums(padded, grad_maps),
            jnp.sum(grad_wide, axis=(0, 1, 2))[None],
            jnp.sum(grad_normed * norm, axis=0)[None],
            jnp.sum(grad_normed, axis=0)[None],
            (gamma * cot_sums)[None],
            moment_row / gamma + b2 * cot_sums,
            pair_b1.reshape(-1, chans),
        ],
        axis=0,
    )
    total_small = total(local_small)
    factor = 1.0 / math.sqrt(pixels * 256)
    param_grads = total_small[:54] * factor
    sums = total_small[54:].reshape(2, 4, 2, 8, 24)
    mine = (core, 0, y_lo, lax.axis_index("z"), 0)
    d_b1 = lax.dynamic_slice(sums, mine, (1, 4, 1, 1, 24)).reshape(shard) * factor
    d_w1, d_w2 = (d_w1 * factor).T, d_w2 * factor
    return (d_input.reshape(block_input.shape), d_w1, d_b1, d_w2, param_grads)


def solution(mesh):
    fine = Mesh(mesh.devices.reshape(SIZES), AXES)
    placed = (
        P(DP, ROWS, None, None),
        P(DP, ROWS, None, None),
        P(),
        P(),
        P(),
        P(),
        P(None, DP),
        P(DP),
        P(DP, None),
        P(),
        P(),
    )
    return jax.shard_map(
        shards,
        mesh=fine,
        in_specs=placed,
        out_specs=(P(DP, ROWS, None, None), P(None, DP), P(DP), P(DP, None), P()),
        check_vma=False,
    )
```

```python
import math

import jax
import jax.numpy as jnp
import numpy as np
from jax import lax
from jax.experimental import pallas as pl
from jax.experimental.pallas import tpu as pltpu
from jax.sharding import Mesh, PartitionSpec as P

KERNEL = 7
MARGIN = 3
EPSILON = 1e-06
INV_ROOT_TWO = 0.7071067811865476
INV_ROOT_TWO_PI = 0.3989422804014327

AXES = ("y_lo", "z", "core", "y_hi", "x")
SIZES = (2, 8, 2, 2, 4)
DP = ("y_lo", "z", "core")
ROWS = ("y_hi", "x")
PAIRS = ("y_lo", "z")
Y = ("y_lo", "y_hi")


def halo(cells):
    down = [(i, i + 1) for i in range(7)]
    up = [(i + 1, i) for i in range(7)]
    above = lax.ppermute(cells[:, -MARGIN:], ROWS, down)
    below = lax.ppermute(cells[:, :MARGIN], ROWS, up)
    return jnp.concatenate([above, cells, below], axis=1)


def swap(cells):
    return lax.ppermute(cells, "core", [(0, 1), (1, 0)])


def spread_sum(part, axes):
    count = lax.axis_size(axes)
    pieces = part.reshape((count, part.shape[0] // count) + part.shape[1:])
    pieces = lax.all_to_all(pieces, axes, 0, 0)
    return jnp.sum(pieces.astype(jnp.float32), axis=0)


def gather(part, axes):
    count = lax.axis_size(axes)
    return lax.all_to_all(jnp.broadcast_to(part[None], (count,) + part.shape), axes, 0, 0)


def total(small):
    size = small.size
    flat = jnp.pad(small.reshape(-1), (0, -size % (16 * 1024))).reshape(16, -1, 128)
    part = spread_sum(flat, ("core",) + ROWS)
    part = jnp.sum(gather(part, PAIRS), axis=0)
    return gather(part, ("core",) + ROWS).reshape(-1)[:size].reshape(small.shape)


def gather_weights(w1_t, w2, b1):
    w2_h = lax.all_gather(w2, PAIRS, axis=0, tiled=True)
    mine = lax.dynamic_slice(w1_t, (lax.axis_index("x") * 24, 0), (24, w1_t.shape[1]))
    bias = jnp.pad(b1[None], ((0, 7), (0, w1_t.shape[1] - b1.shape[0])))
    pieces = gather(gather(jnp.concatenate([mine, bias], axis=0), "z"), "y_lo")
    b1_h = pieces[:, :, 24, : b1.shape[0]].reshape(-1).astype(jnp.float32)
    w1_h = gather(pieces[:, :, :24], "x").transpose(1, 2, 0, 3, 4).reshape(w2_h.shape)
    return w1_h, w2_h, b1_h


def scatter_terms(terms):
    share = lax.psum_scatter(terms, PAIRS, scatter_dimension=0, tiled=True)
    part = spread_sum(share.reshape(-1, LANES), ROWS).astype(jnp.bfloat16)
    return gather(part, ROWS).reshape(share.shape).astype(jnp.float32)


BLOCK = 256
LANES = 128
NT = (((1,), (1,)), ((), ()))
NN = (((1,), (0,)), ((), ()))
TN = (((0,), (0,)), ((), ()))
VMEM = 50 * 2**20


def mlp_kernel(normed, scaled, w1, w2, b1, terms, grad_normed, d_b1, row):
    @pl.when(pl.program_id(0) == 0)
    def _():
        grad_normed[...] = jnp.zeros_like(grad_normed)
        row[...] = jnp.zeros_like(row)

    n, s = normed[...], scaled[...]
    preact = lax.dot_general(w1[...], n, NT, preferred_element_type=jnp.float32) + b1[:, :1]
    cdf = 0.5 * (1.0 + lax.erf(preact * INV_ROOT_TWO))
    hidden = (preact * cdf).astype(jnp.bfloat16)
    slope = cdf + preact * jnp.exp(-0.5 * preact * preact) * INV_ROOT_TWO_PI
    grad_hidden = lax.dot_general(w2[...], s, NT, preferred_element_type=jnp.float32)
    grad_preact = (grad_hidden * slope).astype(jnp.bfloat16)
    total = lax.dot_general(hidden, s, NN, preferred_element_type=jnp.float32)
    terms[:, n.shape[1] :] = total.astype(jnp.bfloat16)
    row[...] += jnp.sum(total * w2[...].astype(jnp.float32), axis=0, keepdims=True)
    terms[:, : n.shape[1]] = lax.dot_general(
        grad_preact, n, NN, preferred_element_type=jnp.float32
    ).astype(jnp.bfloat16)
    d_b1[...] = jnp.broadcast_to(
        jnp.sum(grad_preact.astype(jnp.float32), axis=1, keepdims=True), d_b1.shape
    )
    grad_normed[...] += lax.dot_general(
        grad_preact, w1[...], TN, preferred_element_type=jnp.float32
    )


def mlp(normed, scaled, w1, w2, b1):
    pixels, chans = normed.shape
    hid = w1.shape[0]
    whole = pl.BlockSpec((pixels, chans), lambda i: (0, 0))
    block = pl.BlockSpec((BLOCK, chans), lambda i: (i, 0))
    both = pl.BlockSpec((BLOCK, 2 * chans), lambda i: (i, 0))
    lane = pl.BlockSpec((BLOCK, LANES), lambda i: (i, 0))
    return pl.pallas_call(
        mlp_kernel,
        grid=(hid // BLOCK,),
        in_specs=[whole, whole, block, block, lane],
        out_specs=[both, whole, lane, pl.BlockSpec((1, chans), lambda i: (0, 0))],
        out_shape=[
            jax.ShapeDtypeStruct((hid, 2 * chans), jnp.bfloat16),
            jax.ShapeDtypeStruct((pixels, chans), jnp.float32),
            jax.ShapeDtypeStruct((hid, LANES), jnp.float32),
            jax.ShapeDtypeStruct((1, chans), jnp.float32),
        ],
        compiler_params=pltpu.CompilerParams(vmem_limit_bytes=VMEM),
        cost_estimate=pl.CostEstimate(
            flops=10 * pixels * hid * chans, bytes_accessed=2**24, transcendentals=2 * pixels * hid
        ),
    )(normed, scaled, w1, w2, jnp.broadcast_to(b1[:, None], (hid, LANES)))


def transposed_kernel(padded, cotangent, kernel, d_input, wide):
    rows, cols = d_input.shape[1:3]
    wide[...] = padded[0].astype(jnp.float32)
    for at in range(0, cols, 24):
        sums = [cotangent[0, r, at : at + 24].astype(jnp.float32) for r in range(rows)]
        for b in range(KERNEL):
            column = [(KERNEL - 1 - a) * KERNEL + KERNEL - 1 - b for a in range(KERNEL)]
            taps = [kernel[t : t + 1] for t in column]
            for r in range(rows + KERNEL - 1):
                cells = wide[r, at + b : at + b + 24]
                for a in range(max(0, r - rows + 1), min(KERNEL, r + 1)):
                    sums[r - a] = sums[r - a] + cells * taps[a]
        for r in range(rows):
            d_input[0, r, at : at + 24] = sums[r].astype(jnp.bfloat16)


def transposed(padded, cotangent, kernel):
    images, high, wide, chans = padded.shape
    rows, cols = cotangent.shape[1:3]
    maps = pl.BlockSpec((1, rows, cols, LANES), lambda c, i: (i, 0, 0, c))
    return pl.pallas_call(
        transposed_kernel,
        grid=(chans // LANES, images),
        in_specs=[
            pl.BlockSpec((1, high, wide, LANES), lambda c, i: (i, 0, 0, c)),
            maps,
            pl.BlockSpec((KERNEL * KERNEL, LANES), lambda c, i: (0, c)),
        ],
        out_specs=maps,
        out_shape=jax.ShapeDtypeStruct(cotangent.shape, jnp.bfloat16),
        scratch_shapes=[pltpu.VMEM((high, wide, LANES), jnp.float32)],
        compiler_params=pltpu.CompilerParams(vmem_limit_bytes=VMEM),
        cost_estimate=pl.CostEstimate(
            flops=10**10, bytes_accessed=2**22, transcendentals=0
        ),
    )(padded, cotangent, kernel)


def taps_kernel(padded, grad, sums, wide, grad_wide):
    rows, cols = grad.shape[1:3]
    wide[...] = padded[0].astype(jnp.float32)
    grad_wide[...] = grad[0].astype(jnp.float32)

    @pl.when(pl.program_id(1) == 0)
    def _():
        sums[...] = jnp.zeros_like(sums)

    for b in range(KERNEL):
        totals = [jnp.zeros((8, LANES), jnp.float32) for _ in range(KERNEL)]
        for at in range(0, cols, 16):
            own = [grad_wide[r, at : at + 16] for r in range(rows)]
            for r in range(rows + KERNEL - 1):
                cells = wide[r, at + b : at + b + 16]
                for a in range(max(0, r - rows + 1), min(KERNEL, r + 1)):
                    product = cells * own[r - a]
                    totals[a] = totals[a] + (product[:8] + product[8:])
        for a in range(KERNEL):
            t = a * KERNEL + b
            sums[t : t + 1] += jnp.sum(totals[a], axis=0, keepdims=True)


def tap_sums(padded, grad):
    images, high, wide, chans = padded.shape
    rows, cols = grad.shape[1:3]
    return pl.pallas_call(
        taps_kernel,
        grid=(chans // LANES, images),
        in_specs=[
            pl.BlockSpec((1, high, wide, LANES), lambda c, i: (i, 0, 0, c)),
            pl.BlockSpec((1, rows, cols, LANES), lambda c, i: (i, 0, 0, c)),
        ],
        out_specs=pl.BlockSpec((KERNEL * KERNEL, LANES), lambda c, i: (0, c)),
        out_shape=jax.ShapeDtypeStruct((KERNEL * KERNEL, chans), jnp.float32),
        scratch_shapes=[
            pltpu.VMEM((high, wide, LANES), jnp.float32),
            pltpu.VMEM((rows, cols, LANES), jnp.float32),
        ],
        compiler_params=pltpu.CompilerParams(vmem_limit_bytes=VMEM),
        cost_estimate=pl.CostEstimate(
            flops=10**10, bytes_accessed=2**22, transcendentals=0
        ),
    )(padded, grad)


def pad_columns(cells):
    return jnp.pad(cells, ((0, 0), (0, 0), (MARGIN, 8 - MARGIN), (0, 0)))


def depthwise(padded, kernel, height, width):
    total = jnp.zeros(padded.shape[:-3] + (height, width, padded.shape[-1]), jnp.float32)
    for row_tap in range(KERNEL):
        for col_tap in range(KERNEL):
            window = padded[:, row_tap : row_tap + height, col_tap : col_tap + width]
            total = total + window.astype(jnp.float32) * kernel[row_tap * KERNEL + col_tap]
    return total


def shards(block_input, cotangent, dw_kernel, dw_bias, ln_gain, ln_bias, w1, b1, w2, b2, gamma):
    images, rows_here, cols, chans = block_input.shape
    shard = w1.shape[1]
    pixels = images * rows_here * cols
    flat_cot = cotangent.reshape(pixels, chans).astype(jnp.float32)
    scaled = (flat_cot * gamma).astype(jnp.bfloat16)
    w1_t, w2_h, b1_h = gather_weights(w1.T, w2, b1)

    padded = pad_columns(halo(block_input))
    scaled2 = jnp.concatenate([scaled, swap(scaled)], axis=0)
    conv = depthwise(padded, dw_kernel, rows_here, cols) + dw_bias
    center = conv - jnp.mean(conv, axis=-1, keepdims=True)
    spread = jnp.mean(center * center, axis=-1, keepdims=True)
    rstd = lax.rsqrt(spread + EPSILON).reshape(pixels, 1)
    norm = center.reshape(pixels, chans) * rstd
    normed = (norm * ln_gain + ln_bias).astype(jnp.bfloat16)
    normed2 = jnp.concatenate([normed, swap(normed)], axis=0)

    terms, grad_normed2, sums_b1, moment_row = mlp(normed2, scaled2, w1_t, w2_h, b1_h)
    grad_normed = grad_normed2[:pixels] + swap(grad_normed2[pixels:].astype(jnp.bfloat16)).astype(
        jnp.float32
    )
    share = scatter_terms(terms)

    weighted = grad_normed * ln_gain
    grad_conv = (
        rstd
        * (
            weighted
            - jnp.mean(weighted, axis=-1, keepdims=True)
            - norm * jnp.mean(weighted * norm, axis=-1, keepdims=True)
        )
    ).astype(jnp.bfloat16)
    grad_maps = grad_conv.reshape(block_input.shape)
    grad_padded = pad_columns(halo(grad_maps))
    d_input = transposed(grad_padded, cotangent, dw_kernel)

    grad_wide = grad_maps.astype(jnp.float32)
    cot_sums = jnp.sum(flat_cot, axis=0)
    core = lax.axis_index("core")
    sums_b1 = sums_b1[:, 0][None]
    pair_b1 = jnp.where(core == jnp.arange(2)[:, None], sums_b1, 0.0)
    local_small = jnp.concatenate(
        [
            tap_sums(padded, grad_maps),
            jnp.sum(grad_wide, axis=(0, 1, 2))[None],
            jnp.sum(grad_normed * norm, axis=0)[None],
            jnp.sum(grad_normed, axis=0)[None],
            (gamma * cot_sums)[None],
            moment_row / gamma + b2 * cot_sums,
            pair_b1.reshape(-1, chans),
        ],
        axis=0,
    )
    total_small = total(local_small)
    factor = 1.0 / math.sqrt(pixels * 256)
    param_grads = total_small[:54] * factor
    at = (lax.axis_index("y_lo") * 8 + lax.axis_index("z")) * shard
    sums = total_small[54:].reshape(2, -1)
    d_b1 = lax.dynamic_slice(sums, (core, at), (1, shard)).reshape(shard) * factor
    share = share * factor
    d_w1, d_w2 = share[:, :chans].T, share[:, chans:]
    return (d_input.reshape(block_input.shape), d_w1, d_b1, d_w2, param_grads)


def solution(mesh):
    fine = Mesh(mesh.devices.reshape(SIZES), AXES)
    placed = (
        P(DP, ROWS, None, None),
        P(DP, ROWS, None, None),
        P(),
        P(),
        P(),
        P(),
        P(None, DP),
        P(DP),
        P(DP, None),
        P(),
        P(),
    )
    return jax.shard_map(
        shards,
        mesh=fine,
        in_specs=placed,
        out_specs=(P(DP, ROWS, None, None), P(None, DP), P(DP), P(DP, None), P()),
        check_vma=False,
    )
```

```python
import math

import jax
import jax.numpy as jnp
import numpy as np
from jax import lax
from jax.experimental import pallas as pl
from jax.experimental.pallas import tpu as pltpu
from jax.sharding import Mesh, PartitionSpec as P

KERNEL = 7
MARGIN = 3
EPSILON = 1e-06
INV_ROOT_TWO = 0.7071067811865476
INV_ROOT_TWO_PI = 0.3989422804014327

AXES = ("y_lo", "z", "core", "y_hi", "x")
SIZES = (2, 8, 2, 2, 4)
DP = ("y_lo", "z", "core")
ROWS = ("y_hi", "x")
PAIRS = ("y_lo", "z")
Y = ("y_lo", "y_hi")


def halo(cells):
    down = [(i, i + 1) for i in range(7)]
    up = [(i + 1, i) for i in range(7)]
    above = lax.ppermute(cells[:, -MARGIN:], ROWS, down)
    below = lax.ppermute(cells[:, :MARGIN], ROWS, up)
    return jnp.concatenate([above, cells, below], axis=1)


def swap(cells):
    return lax.ppermute(cells, "core", [(0, 1), (1, 0)])


def spread_sum(part, axes):
    count = lax.axis_size(axes)
    pieces = part.reshape((count, part.shape[0] // count) + part.shape[1:])
    pieces = lax.all_to_all(pieces, axes, 0, 0)
    return jnp.sum(pieces.astype(jnp.float32), axis=0)


def gather(part, axes):
    count = lax.axis_size(axes)
    return lax.all_to_all(jnp.broadcast_to(part[None], (count,) + part.shape), axes, 0, 0)


def shift(cells, ring, step):
    if ring == "x":
        return lax.ppermute(cells, "x", [(i, (i + step) % 4) for i in range(4)])
    place = [(y % 2) * 2 + y // 2 for y in range(4)]
    return lax.ppermute(cells, Y, [(place[y], place[(y + step) % 4]) for y in range(4)])


def ring_gather(mine, ring):
    half = mine.shape[0] // 2
    left = shift(mine, ring, 1)
    right = shift(mine, ring, -1)
    far = [shift(left[:half], ring, 1), shift(right[half:], ring, -1)]
    return [mine, right, jnp.concatenate(far, axis=0), left]


def ring_sum(parts, ring):
    half = parts[2].shape[0] // 2
    wide = [part.astype(jnp.float32) for part in parts]
    up = shift(parts[2][:half], ring, 1).astype(jnp.float32)
    down = shift(parts[2][half:], ring, -1).astype(jnp.float32)
    right = jnp.concatenate([wide[1][:half] + up, wide[1][half:]], axis=0)
    left = jnp.concatenate([wide[3][:half], wide[3][half:] + down], axis=0)
    right = shift(right.astype(jnp.bfloat16), ring, 1)
    left = shift(left.astype(jnp.bfloat16), ring, -1)
    return wide[0] + right.astype(jnp.float32) + left.astype(jnp.float32)


def y_flags():
    y = lax.axis_index("y_hi") * 2 + lax.axis_index("y_lo")
    return y // 2 == 1, ((y + 1) % 4) // 2 == 1


def join(one, other, second):
    return jnp.where(
        second,
        jnp.concatenate([other, one], axis=1),
        jnp.concatenate([one, other], axis=1),
    )


def cut(cells, second):
    low, high = cells[:, :384], cells[:, 384:]
    return jnp.where(second, high, low), jnp.where(second, low, high)


def gather_z(w1_t, w2, b1):
    x, y_hi = lax.axis_index("x"), lax.axis_index("y_hi")
    mine = [lax.dynamic_slice(w, (x * 24, y_hi * 384), (24, 384)) for w in (w1_t, w2)]
    bias = jnp.pad(b1[None], ((0, 7), (0, 384 - b1.shape[0])))
    return gather(jnp.concatenate(mine + [bias], axis=0), "z")


def gather_weights(along_z):
    first = along_z[:, :24].reshape(192, 384)
    second = along_z[:, 24:48].reshape(192, 384)
    here, there = y_flags()
    second = gather(second, "x").reshape(768, 384)
    first = [first] + [shift(first, "y", -k) for k in (1, 2, 3)]
    first = jnp.concatenate(
        [join(first[0], first[2], here), join(first[1], first[3], there)], axis=0
    )
    second = ring_gather(second, "y")
    first = gather(first, "x").reshape(-1, 768)
    second = jnp.stack(
        [
            join(second[0], second[2], here).reshape(4, 192, 768),
            join(second[1], second[3], there).reshape(4, 192, 768),
        ],
        axis=1,
    ).reshape(-1, 768)
    bias = along_z[:, 48, :96]
    bias = jnp.stack([bias, shift(bias, "y", 1)]).reshape(2, 8, 4, 24).astype(jnp.float32)
    return first, second, bias.transpose(2, 0, 1, 3).reshape(-1)


def scatter_terms(term_w1, moment):
    here, there = y_flags()
    moment = moment.reshape(4, 2, 192, 768)
    near = cut(moment[:, 0].reshape(768, 768), here)
    next_to = cut(moment[:, 1].reshape(768, 768), there)
    second = ring_sum([near[0], next_to[0], near[1], next_to[1]], "y")
    first = spread_sum(term_w1, "x").astype(jnp.bfloat16)
    second = spread_sum(second.astype(jnp.bfloat16), "x")
    near, next_to = cut(first[:192], here), cut(first[192:], there)
    sent = [next_to[0], near[1], next_to[1]]
    first = near[0].astype(jnp.float32)
    for k in (1, 2, 3):
        first = first + shift(sent[k - 1], "y", k).astype(jnp.float32)
    return jnp.concatenate([first, second], axis=1).reshape(8, 24, 768)


def finish(terms, small):
    small = small + swap(small)
    small = small + lax.ppermute(small, "y_lo", [(0, 1), (1, 0)])
    small = spread_sum(small, ROWS)
    small = jnp.broadcast_to(small[None], (8,) + small.shape)
    pieces = jnp.concatenate([terms, small], axis=1)
    total = gather(jnp.sum(lax.all_to_all(pieces, "z", 0, 0), axis=0), ROWS)
    blocks = total[:, :24].reshape(2, 4, 24, 2, 384).transpose(3, 1, 2, 0, 4).reshape(2, 96, 768)
    return blocks[0], blocks[1], total[:, 24:].reshape(-1, 768)


BLOCK = 256
LANES = 128
NT = (((1,), (1,)), ((), ()))
NN = (((1,), (0,)), ((), ()))
TN = (((0,), (0,)), ((), ()))
VMEM = 50 * 2**20


def mlp_kernel(normed, scaled, w1, w2, b1, d_w1, moment, grad_normed, d_b1, row):
    @pl.when(pl.program_id(0) == 0)
    def _():
        grad_normed[...] = jnp.zeros_like(grad_normed)
        row[...] = jnp.zeros_like(row)

    n, s = normed[...], scaled[...]
    preact = lax.dot_general(w1[...], n, NT, preferred_element_type=jnp.float32) + b1[:, :1]
    cdf = 0.5 * (1.0 + lax.erf(preact * INV_ROOT_TWO))
    hidden = (preact * cdf).astype(jnp.bfloat16)
    slope = cdf + preact * jnp.exp(-0.5 * preact * preact) * INV_ROOT_TWO_PI
    grad_hidden = lax.dot_general(w2[...], s, NT, preferred_element_type=jnp.float32)
    grad_preact = (grad_hidden * slope).astype(jnp.bfloat16)
    total = lax.dot_general(hidden, s, NN, preferred_element_type=jnp.float32)
    moment[...] = total.astype(jnp.bfloat16)
    row[...] += jnp.sum(total * w2[...].astype(jnp.float32), axis=0, keepdims=True)
    d_w1[...] = lax.dot_general(grad_preact, n, NN, preferred_element_type=jnp.float32).astype(
        jnp.bfloat16
    )
    d_b1[...] = jnp.broadcast_to(
        jnp.sum(grad_preact.astype(jnp.float32), axis=1, keepdims=True), d_b1.shape
    )
    grad_normed[...] += lax.dot_general(
        grad_preact, w1[...], TN, preferred_element_type=jnp.float32
    )


def mlp(normed, scaled, w1, w2, b1):
    pixels, chans = normed.shape
    hid = w1.shape[0]
    whole = pl.BlockSpec((pixels, chans), lambda i: (0, 0))
    block = pl.BlockSpec((BLOCK, chans), lambda i: (i, 0))
    lane = pl.BlockSpec((BLOCK, LANES), lambda i: (i, 0))
    return pl.pallas_call(
        mlp_kernel,
        grid=(hid // BLOCK,),
        in_specs=[whole, whole, block, block, lane],
        out_specs=[block, block, whole, lane, pl.BlockSpec((1, chans), lambda i: (0, 0))],
        out_shape=[
            jax.ShapeDtypeStruct((hid, chans), jnp.bfloat16),
            jax.ShapeDtypeStruct((hid, chans), jnp.bfloat16),
            jax.ShapeDtypeStruct((pixels, chans), jnp.float32),
            jax.ShapeDtypeStruct((hid, LANES), jnp.float32),
            jax.ShapeDtypeStruct((1, chans), jnp.float32),
        ],
        compiler_params=pltpu.CompilerParams(vmem_limit_bytes=VMEM),
        cost_estimate=pl.CostEstimate(
            flops=10 * pixels * hid * chans, bytes_accessed=2**24, transcendentals=2 * pixels * hid
        ),
    )(normed, scaled, w1, w2, jnp.broadcast_to(b1[:, None], (hid, LANES)))


def transposed_kernel(padded, cotangent, kernel, d_input, wide):
    rows, cols = d_input.shape[1:3]
    wide[...] = padded[0].astype(jnp.float32)
    for at in range(0, cols, 24):
        sums = [cotangent[0, r, at : at + 24].astype(jnp.float32) for r in range(rows)]
        for b in range(KERNEL):
            column = [(KERNEL - 1 - a) * KERNEL + KERNEL - 1 - b for a in range(KERNEL)]
            taps = [kernel[t : t + 1] for t in column]
            for r in range(rows + KERNEL - 1):
                cells = wide[r, at + b : at + b + 24]
                for a in range(max(0, r - rows + 1), min(KERNEL, r + 1)):
                    sums[r - a] = sums[r - a] + cells * taps[a]
        for r in range(rows):
            d_input[0, r, at : at + 24] = sums[r].astype(jnp.bfloat16)


def transposed(padded, cotangent, kernel):
    images, high, wide, chans = padded.shape
    rows, cols = cotangent.shape[1:3]
    maps = pl.BlockSpec((1, rows, cols, LANES), lambda c, i: (i, 0, 0, c))
    return pl.pallas_call(
        transposed_kernel,
        grid=(chans // LANES, images),
        in_specs=[
            pl.BlockSpec((1, high, wide, LANES), lambda c, i: (i, 0, 0, c)),
            maps,
            pl.BlockSpec((KERNEL * KERNEL, LANES), lambda c, i: (0, c)),
        ],
        out_specs=maps,
        out_shape=jax.ShapeDtypeStruct(cotangent.shape, jnp.bfloat16),
        scratch_shapes=[pltpu.VMEM((high, wide, LANES), jnp.float32)],
        compiler_params=pltpu.CompilerParams(vmem_limit_bytes=VMEM),
        cost_estimate=pl.CostEstimate(
            flops=10**10, bytes_accessed=2**22, transcendentals=0
        ),
    )(padded, cotangent, kernel)


def taps_kernel(padded, grad, sums, wide, grad_wide):
    rows, cols = grad.shape[1:3]
    wide[...] = padded[0].astype(jnp.float32)
    grad_wide[...] = grad[0].astype(jnp.float32)

    @pl.when(pl.program_id(1) == 0)
    def _():
        sums[...] = jnp.zeros_like(sums)

    for b in range(KERNEL):
        totals = [jnp.zeros((8, LANES), jnp.float32) for _ in range(KERNEL)]
        for at in range(0, cols, 16):
            own = [grad_wide[r, at : at + 16] for r in range(rows)]
            for r in range(rows + KERNEL - 1):
                cells = wide[r, at + b : at + b + 16]
                for a in range(max(0, r - rows + 1), min(KERNEL, r + 1)):
                    product = cells * own[r - a]
                    totals[a] = totals[a] + (product[:8] + product[8:])
        for a in range(KERNEL):
            t = a * KERNEL + b
            sums[t : t + 1] += jnp.sum(totals[a], axis=0, keepdims=True)


def tap_sums(padded, grad):
    images, high, wide, chans = padded.shape
    rows, cols = grad.shape[1:3]
    return pl.pallas_call(
        taps_kernel,
        grid=(chans // LANES, images),
        in_specs=[
            pl.BlockSpec((1, high, wide, LANES), lambda c, i: (i, 0, 0, c)),
            pl.BlockSpec((1, rows, cols, LANES), lambda c, i: (i, 0, 0, c)),
        ],
        out_specs=pl.BlockSpec((KERNEL * KERNEL, LANES), lambda c, i: (0, c)),
        out_shape=jax.ShapeDtypeStruct((KERNEL * KERNEL, chans), jnp.float32),
        scratch_shapes=[
            pltpu.VMEM((high, wide, LANES), jnp.float32),
            pltpu.VMEM((rows, cols, LANES), jnp.float32),
        ],
        compiler_params=pltpu.CompilerParams(vmem_limit_bytes=VMEM),
        cost_estimate=pl.CostEstimate(
            flops=10**10, bytes_accessed=2**22, transcendentals=0
        ),
    )(padded, grad)


def pad_columns(cells):
    return jnp.pad(cells, ((0, 0), (0, 0), (MARGIN, 8 - MARGIN), (0, 0)))


def depthwise(padded, kernel, height, width):
    total = jnp.zeros(padded.shape[:-3] + (height, width, padded.shape[-1]), jnp.float32)
    for row_tap in range(KERNEL):
        for col_tap in range(KERNEL):
            window = padded[:, row_tap : row_tap + height, col_tap : col_tap + width]
            total = total + window.astype(jnp.float32) * kernel[row_tap * KERNEL + col_tap]
    return total


def shards(block_input, cotangent, dw_kernel, dw_bias, ln_gain, ln_bias, w1, b1, w2, b2, gamma):
    images, rows_here, cols, chans = block_input.shape
    shard = w1.shape[1]
    pixels = images * rows_here * cols
    flat_cot = cotangent.reshape(pixels, chans).astype(jnp.float32)
    scaled = (flat_cot * gamma).astype(jnp.bfloat16)
    along_z = gather_z(w1.T, w2, b1)

    padded, along_z = lax.optimization_barrier((halo(block_input), along_z))
    padded = pad_columns(padded)
    w1_t, w2_h, b1_h = gather_weights(along_z)
    scaled2 = jnp.concatenate([scaled, swap(scaled)], axis=0)
    conv = depthwise(padded, dw_kernel, rows_here, cols) + dw_bias
    center = conv - jnp.mean(conv, axis=-1, keepdims=True)
    spread = jnp.mean(center * center, axis=-1, keepdims=True)
    rstd = lax.rsqrt(spread + EPSILON).reshape(pixels, 1)
    norm = center.reshape(pixels, chans) * rstd
    normed = (norm * ln_gain + ln_bias).astype(jnp.bfloat16)
    normed2 = jnp.concatenate([normed, swap(normed)], axis=0)

    term_w1, moment, grad_normed2, sums_b1, moment_row = mlp(normed2, scaled2, w1_t, w2_h, b1_h)
    grad_normed = grad_normed2[:pixels] + swap(grad_normed2[pixels:].astype(jnp.bfloat16)).astype(
        jnp.float32
    )
    terms = scatter_terms(term_w1, moment)

    weighted = grad_normed * ln_gain
    grad_conv = (
        rstd
        * (
            weighted
            - jnp.mean(weighted, axis=-1, keepdims=True)
            - norm * jnp.mean(weighted * norm, axis=-1, keepdims=True)
        )
    ).astype(jnp.bfloat16)
    grad_maps = grad_conv.reshape(block_input.shape)
    grad_padded = pad_columns(halo(grad_maps))
    d_input = transposed(grad_padded, cotangent, dw_kernel)

    grad_wide = grad_maps.astype(jnp.float32)
    cot_sums = jnp.sum(flat_cot, axis=0)
    core = lax.axis_index("core")
    y_lo = lax.axis_index("y_lo")
    sums_b1 = jnp.roll(sums_b1[:, 0].reshape(4, 2, 8, 24), y_lo, 1).reshape(1, -1)
    pair_b1 = jnp.where(core == jnp.arange(2)[:, None], sums_b1, 0.0)
    local_small = jnp.concatenate(
        [
            tap_sums(padded, grad_maps),
            jnp.sum(grad_wide, axis=(0, 1, 2))[None],
            jnp.sum(grad_normed * norm, axis=0)[None],
            jnp.sum(grad_normed, axis=0)[None],
            (gamma * cot_sums)[None],
            moment_row / gamma + b2 * cot_sums,
            pair_b1.reshape(-1, chans),
            jnp.zeros((6, chans), jnp.float32),
        ],
        axis=0,
    )
    d_w1, d_w2, total_small = finish(terms, local_small)
    factor = 1.0 / math.sqrt(pixels * 256)
    param_grads = total_small[:54] * factor
    sums = total_small[54:58].reshape(2, 4, 2, 8, 24)
    mine = (core, 0, y_lo, lax.axis_index("z"), 0)
    d_b1 = lax.dynamic_slice(sums, mine, (1, 4, 1, 1, 24)).reshape(shard) * factor
    d_w1, d_w2 = (d_w1 * factor).T, d_w2 * factor
    return (d_input.reshape(block_input.shape), d_w1, d_b1, d_w2, param_grads)


def solution(mesh):
    fine = Mesh(mesh.devices.reshape(SIZES), AXES)
    placed = (
        P(DP, ROWS, None, None),
        P(DP, ROWS, None, None),
        P(),
        P(),
        P(),
        P(),
        P(None, DP),
        P(DP),
        P(DP, None),
        P(),
        P(),
    )
    return jax.shard_map(
        shards,
        mesh=fine,
        in_specs=placed,
        out_specs=(P(DP, ROWS, None, None), P(None, DP), P(DP), P(DP, None), P()),
        check_vma=False,
    )
```

```python
import math

import jax
import jax.numpy as jnp
import numpy as np
from jax import lax
from jax.experimental import pallas as pl
from jax.experimental.pallas import tpu as pltpu
from jax.sharding import Mesh, PartitionSpec as P

KERNEL = 7
MARGIN = 3
EPSILON = 1e-06
INV_ROOT_TWO = 0.7071067811865476
INV_ROOT_TWO_PI = 0.3989422804014327

AXES = ("y_lo", "z", "core", "y_hi", "x")
SIZES = (2, 8, 2, 2, 4)
DP = ("y_lo", "z", "core")
ROWS = ("y_hi", "x")
PAIRS = ("y_lo", "z")
Y = ("y_lo", "y_hi")


def halo(cells):
    down = [(i, i + 1) for i in range(7)]
    up = [(i + 1, i) for i in range(7)]
    above = lax.ppermute(cells[:, -MARGIN:], ROWS, down)
    below = lax.ppermute(cells[:, :MARGIN], ROWS, up)
    return jnp.concatenate([above, cells, below], axis=1)


def swap(cells):
    return lax.ppermute(cells, "core", [(0, 1), (1, 0)])


def spread_sum(part, axes):
    count = lax.axis_size(axes)
    pieces = part.reshape((count, part.shape[0] // count) + part.shape[1:])
    pieces = lax.all_to_all(pieces, axes, 0, 0)
    return jnp.sum(pieces.astype(jnp.float32), axis=0)


def gather(part, axes):
    count = lax.axis_size(axes)
    return lax.all_to_all(jnp.broadcast_to(part[None], (count,) + part.shape), axes, 0, 0)


def across(cells, m):
    flip = (m % 2) * 2 + m // 2
    return lax.ppermute(cells, Y, [(i, i ^ flip) for i in range(4)])


def relative(cells):
    half = cells.shape[-1] // 2
    turned = jnp.concatenate([cells[..., half:], cells[..., :half]], axis=-1)
    return jnp.where(lax.axis_index("y_hi") == 1, turned, cells)


def gather_z(w1_t, w2, b1):
    x, y_hi = lax.axis_index("x"), lax.axis_index("y_hi")
    mine = [lax.dynamic_slice(w, (x * 24, y_hi * 384), (24, 384)) for w in (w1_t, w2)]
    bias = jnp.pad(b1[None], ((0, 7), (0, 384 - b1.shape[0])))
    return gather(jnp.concatenate(mine + [bias], axis=0), "z")


def gather_w1(along_z):
    part = along_z[:, :24].reshape(192, 384)
    near, far, last = [across(part, m) for m in (1, 2, 3)]
    whole = jnp.concatenate(
        [jnp.concatenate([part, far], axis=1), jnp.concatenate([near, last], axis=1)], axis=0
    )
    return gather(whole, "x").reshape(-1, 768)


def gather_w2(part):
    half = part.shape[0] // 2
    near, last = across(part, 1), across(part, 3)
    far = jnp.concatenate([across(last[:half], 1), across(near[half:], 3)], axis=0)
    return part, near, far, last


def gather_b1(along_z):
    bias = along_z[:, 48, :96]
    bias = jnp.stack([bias, across(bias, 1)]).reshape(2, 8, 4, 24).astype(jnp.float32)
    return bias.transpose(2, 0, 1, 3).reshape(-1)


def scatter_terms(d_w1, parts):
    own, near, far, last = parts
    half = far.shape[0] // 2
    up = across(far[:half], 1).astype(jnp.float32)
    down = across(far[half:], 3).astype(jnp.float32)
    last = jnp.concatenate(
        [(last[:half].astype(jnp.float32) + up).astype(jnp.bfloat16), last[half:]], axis=0
    )
    near = jnp.concatenate(
        [near[:half], (near[half:].astype(jnp.float32) + down).astype(jnp.bfloat16)], axis=0
    )
    second = own.astype(jnp.float32)
    second = second + across(near, 1).astype(jnp.float32) + across(last, 3).astype(jnp.float32)
    first = spread_sum(d_w1, "x").astype(jnp.bfloat16)
    first, second = lax.optimization_barrier((first, second.astype(jnp.bfloat16)))
    second = spread_sum(second, "x")
    sent = (first[192:, :384], first[:192, 384:], first[192:, 384:])
    first = first[:192, :384].astype(jnp.float32)
    for m in (1, 2, 3):
        first = first + across(sent[m - 1], m).astype(jnp.float32)
    return first, second


def two(cells):
    high = lax.reduce_precision(cells, 8, 7)
    return jnp.concatenate([high, cells - high], axis=0).astype(jnp.bfloat16)


def finish(first, second, small):
    small = small + swap(small)
    small = small + lax.ppermute(small, "y_lo", [(0, 1), (1, 0)])
    first, second, small = lax.optimization_barrier((first, second, small))
    small = two(spread_sum(small, ROWS))
    terms = jnp.concatenate([first, second], axis=1).astype(jnp.bfloat16).reshape(8, 24, 768)
    small = jnp.broadcast_to(small[None], (8,) + small.shape)
    pieces = lax.all_to_all(jnp.concatenate([terms, small], axis=1), "z", 0, 0)
    total = jnp.sum(pieces.astype(jnp.float32), axis=0)
    small = total[24:32] + total[32:]
    total = gather(jnp.concatenate([total[:24].astype(jnp.bfloat16), two(small)], axis=0), ROWS)
    total = total.astype(jnp.float32)
    blocks = total[:, :24].reshape(2, 4, 24, 2, 384).transpose(3, 1, 2, 0, 4).reshape(2, 96, 768)
    return blocks[0], blocks[1], (total[:, 24:32] + total[:, 32:]).reshape(-1, 768)


BLOCK = 384
LANES = 128
NT = (((1,), (1,)), ((), ()))
NN = (((1,), (0,)), ((), ()))
TN = (((0,), (0,)), ((), ()))
VMEM = 56 * 2**20


def mlp_kernel(
    normed, scaled, w1, q0, q1, q2, q3, b1, d_w1, m0, m1, m2, m3, own, peer, d_b1, row, sums
):
    @pl.when(pl.program_id(0) == 0)
    def _():
        sums[...] = jnp.zeros_like(sums)
        row[...] = jnp.zeros_like(row)

    n, s = normed[...], scaled[...]
    high, wide = q0.shape
    w2 = jnp.concatenate(
        [
            jnp.concatenate([q0[...], q2[...]], axis=1),
            jnp.concatenate([q1[...], q3[...]], axis=1),
        ],
        axis=0,
    )
    preact = lax.dot_general(w1[...], n, NT, preferred_element_type=jnp.float32) + b1[:, :1]
    cdf = 0.5 * (1.0 + lax.erf(preact * INV_ROOT_TWO))
    hidden = (preact * cdf).astype(jnp.bfloat16)
    slope = cdf + preact * jnp.exp(-0.5 * preact * preact) * INV_ROOT_TWO_PI
    grad_hidden = lax.dot_general(w2, s, NT, preferred_element_type=jnp.float32)
    grad_preact = (grad_hidden * slope).astype(jnp.bfloat16)
    d_w1[...] = lax.dot_general(grad_preact, n, NN, preferred_element_type=jnp.float32).astype(
        jnp.bfloat16
    )
    moment = lax.dot_general(hidden, s, NN, preferred_element_type=jnp.float32)
    m0[...] = moment[:high, :wide].astype(jnp.bfloat16)
    m1[...] = moment[high:, :wide].astype(jnp.bfloat16)
    m2[...] = moment[:high, wide:].astype(jnp.bfloat16)
    m3[...] = moment[high:, wide:].astype(jnp.bfloat16)
    row[...] += jnp.sum(moment * w2.astype(jnp.float32), axis=0, keepdims=True)
    d_b1[...] = jnp.broadcast_to(
        jnp.sum(grad_preact.astype(jnp.float32), axis=1, keepdims=True), d_b1.shape
    )
    sums[...] += lax.dot_general(grad_preact, w1[...], TN, preferred_element_type=jnp.float32)

    @pl.when(pl.program_id(0) == pl.num_programs(0) - 1)
    def _():
        half = own.shape[0]
        own[...] = sums[:half]
        peer[...] = sums[half:].astype(jnp.bfloat16)


def mlp(normed, scaled, w1, parts, b1):
    pixels, chans = normed.shape
    hid = w1.shape[0]
    whole = pl.BlockSpec((pixels, chans), lambda i: (0, 0))
    half = pl.BlockSpec((pixels // 2, chans), lambda i: (0, 0))
    block = pl.BlockSpec((BLOCK, chans), lambda i: (i, 0))
    part = pl.BlockSpec((BLOCK // 2, chans // 2), lambda i: (i, 0))
    lane = pl.BlockSpec((BLOCK, LANES), lambda i: (i, 0))
    return pl.pallas_call(
        mlp_kernel,
        grid=(hid // BLOCK,),
        in_specs=[whole, whole, block] + [part] * 4 + [lane],
        out_specs=[block] + [part] * 4 + [half, half, lane, pl.BlockSpec((1, chans), lambda i: (0, 0))],
        out_shape=[jax.ShapeDtypeStruct((hid, chans), jnp.bfloat16)]
        + [jax.ShapeDtypeStruct((hid // 2, chans // 2), jnp.bfloat16)] * 4
        + [
            jax.ShapeDtypeStruct((pixels // 2, chans), jnp.float32),
            jax.ShapeDtypeStruct((pixels // 2, chans), jnp.bfloat16),
            jax.ShapeDtypeStruct((hid, LANES), jnp.float32),
            jax.ShapeDtypeStruct((1, chans), jnp.float32),
        ],
        scratch_shapes=[pltpu.VMEM((pixels, chans), jnp.float32)],
        compiler_params=pltpu.CompilerParams(vmem_limit_bytes=VMEM),
        cost_estimate=pl.CostEstimate(
            flops=10 * pixels * hid * chans, bytes_accessed=2**24, transcendentals=2 * pixels * hid
        ),
    )(normed, scaled, w1, *parts, jnp.broadcast_to(b1[:, None], (hid, LANES)))


def transposed_kernel(padded, cotangent, kernel, d_input, wide):
    rows, cols = d_input.shape[1:3]
    wide[...] = padded[0].astype(jnp.float32)
    for at in range(0, cols, 24):
        sums = [cotangent[0, r, at : at + 24].astype(jnp.float32) for r in range(rows)]
        for b in range(KERNEL):
            column = [(KERNEL - 1 - a) * KERNEL + KERNEL - 1 - b for a in range(KERNEL)]
            taps = [kernel[t : t + 1] for t in column]
            for r in range(rows + KERNEL - 1):
                cells = wide[r, at + b : at + b + 24]
                for a in range(max(0, r - rows + 1), min(KERNEL, r + 1)):
                    sums[r - a] = sums[r - a] + cells * taps[a]
        for r in range(rows):
            d_input[0, r, at : at + 24] = sums[r].astype(jnp.bfloat16)


def transposed(padded, cotangent, kernel):
    images, high, wide, chans = padded.shape
    rows, cols = cotangent.shape[1:3]
    maps = pl.BlockSpec((1, rows, cols, LANES), lambda c, i: (i, 0, 0, c))
    return pl.pallas_call(
        transposed_kernel,
        grid=(chans // LANES, images),
        in_specs=[
            pl.BlockSpec((1, high, wide, LANES), lambda c, i: (i, 0, 0, c)),
            maps,
            pl.BlockSpec((KERNEL * KERNEL, LANES), lambda c, i: (0, c)),
        ],
        out_specs=maps,
        out_shape=jax.ShapeDtypeStruct(cotangent.shape, jnp.bfloat16),
        scratch_shapes=[pltpu.VMEM((high, wide, LANES), jnp.float32)],
        compiler_params=pltpu.CompilerParams(vmem_limit_bytes=VMEM),
        cost_estimate=pl.CostEstimate(
            flops=10**10, bytes_accessed=2**22, transcendentals=0
        ),
    )(padded, cotangent, kernel)


def taps_kernel(padded, grad, sums, wide, grad_wide):
    rows, cols = grad.shape[1:3]
    wide[...] = padded[0].astype(jnp.float32)
    grad_wide[...] = grad[0].astype(jnp.float32)

    @pl.when(pl.program_id(1) == 0)
    def _():
        sums[...] = jnp.zeros_like(sums)

    for b in range(KERNEL):
        totals = [jnp.zeros((8, LANES), jnp.float32) for _ in range(KERNEL)]
        for at in range(0, cols, 16):
            own = [grad_wide[r, at : at + 16] for r in range(rows)]
            for r in range(rows + KERNEL - 1):
                cells = wide[r, at + b : at + b + 16]
                for a in range(max(0, r - rows + 1), min(KERNEL, r + 1)):
                    product = cells * own[r - a]
                    totals[a] = totals[a] + (product[:8] + product[8:])
        for a in range(KERNEL):
            t = a * KERNEL + b
            sums[t : t + 1] += jnp.sum(totals[a], axis=0, keepdims=True)


def tap_sums(padded, grad):
    images, high, wide, chans = padded.shape
    rows, cols = grad.shape[1:3]
    return pl.pallas_call(
        taps_kernel,
        grid=(chans // LANES, images),
        in_specs=[
            pl.BlockSpec((1, high, wide, LANES), lambda c, i: (i, 0, 0, c)),
            pl.BlockSpec((1, rows, cols, LANES), lambda c, i: (i, 0, 0, c)),
        ],
        out_specs=pl.BlockSpec((KERNEL * KERNEL, LANES), lambda c, i: (0, c)),
        out_shape=jax.ShapeDtypeStruct((KERNEL * KERNEL, chans), jnp.float32),
        scratch_shapes=[
            pltpu.VMEM((high, wide, LANES), jnp.float32),
            pltpu.VMEM((rows, cols, LANES), jnp.float32),
        ],
        compiler_params=pltpu.CompilerParams(vmem_limit_bytes=VMEM),
        cost_estimate=pl.CostEstimate(
            flops=10**10, bytes_accessed=2**22, transcendentals=0
        ),
    )(padded, grad)


def pad_columns(cells):
    return jnp.pad(cells, ((0, 0), (0, 0), (MARGIN, 8 - MARGIN), (0, 0)))


def depthwise(padded, kernel, height, width):
    total = jnp.zeros(padded.shape[:-3] + (height, width, padded.shape[-1]), jnp.float32)
    for row_tap in range(KERNEL):
        for col_tap in range(KERNEL):
            window = padded[:, row_tap : row_tap + height, col_tap : col_tap + width]
            total = total + window.astype(jnp.float32) * kernel[row_tap * KERNEL + col_tap]
    return total


def shards(block_input, cotangent, dw_kernel, dw_bias, ln_gain, ln_bias, w1, b1, w2, b2, gamma):
    images, rows_here, cols, chans = block_input.shape
    shard = w1.shape[1]
    pixels = images * rows_here * cols
    flat_cot = cotangent.reshape(pixels, chans).astype(jnp.float32)
    scaled = (flat_cot * gamma).astype(jnp.bfloat16)
    along_z = gather_z(w1.T, w2, b1)
    maps, along_z = lax.optimization_barrier((block_input, along_z))
    w2_part = gather(along_z[:, 24:48].reshape(192, 384), "x").reshape(768, 384)
    w1_h = gather_w1(along_z)
    b1_h = gather_b1(along_z)
    padded, w2_part = lax.optimization_barrier((halo(maps), w2_part))
    padded = pad_columns(padded)
    w2_parts = gather_w2(w2_part)
    scaled = relative(scaled)
    scaled2 = jnp.concatenate([scaled, swap(scaled)], axis=0)
    conv = depthwise(padded, dw_kernel, rows_here, cols) + dw_bias
    center = conv - jnp.mean(conv, axis=-1, keepdims=True)
    spread = jnp.mean(center * center, axis=-1, keepdims=True)
    rstd = lax.rsqrt(spread + EPSILON).reshape(pixels, 1)
    norm = center.reshape(pixels, chans) * rstd
    normed = (norm * ln_gain + ln_bias).astype(jnp.bfloat16)
    normed = relative(normed)
    normed2 = jnp.concatenate([normed, swap(normed)], axis=0)

    d_w1, *parts, own, peer, sums_b1, moment_row = mlp(normed2, scaled2, w1_h, w2_parts, b1_h)
    first, second = scatter_terms(d_w1, parts)
    grad_normed = relative(own + swap(peer).astype(jnp.float32))
    moment_row = relative(moment_row)

    weighted = grad_normed * ln_gain
    grad_conv = (
        rstd
        * (
            weighted
            - jnp.mean(weighted, axis=-1, keepdims=True)
            - norm * jnp.mean(weighted * norm, axis=-1, keepdims=True)
        )
    ).astype(jnp.bfloat16)
    grad_maps = grad_conv.reshape(block_input.shape)
    grad_padded = pad_columns(halo(grad_maps))
    d_input = transposed(grad_padded, cotangent, dw_kernel)

    grad_wide = grad_maps.astype(jnp.float32)
    cot_sums = jnp.sum(flat_cot, axis=0)
    core = lax.axis_index("core")
    y_lo = lax.axis_index("y_lo")
    sums_b1 = jnp.roll(sums_b1[:, 0].reshape(4, 2, 8, 24), y_lo, 1).reshape(1, -1)
    pair_b1 = jnp.where(core == jnp.arange(2)[:, None], sums_b1, 0.0)
    local_small = jnp.concatenate(
        [
            tap_sums(padded, grad_maps),
            jnp.sum(grad_wide, axis=(0, 1, 2))[None],
            jnp.sum(grad_normed * norm, axis=0)[None],
            jnp.sum(grad_normed, axis=0)[None],
            (gamma * cot_sums)[None],
            moment_row / gamma + b2 * cot_sums,
            pair_b1.reshape(-1, chans),
            jnp.zeros((6, chans), jnp.float32),
        ],
        axis=0,
    )
    d_w1, d_w2, total_small = finish(first, second, local_small)
    factor = 1.0 / math.sqrt(pixels * 256)
    param_grads = total_small[:54] * factor
    sums = total_small[54:58].reshape(2, 4, 2, 8, 24)
    mine = (core, 0, y_lo, lax.axis_index("z"), 0)
    d_b1 = lax.dynamic_slice(sums, mine, (1, 4, 1, 1, 24)).reshape(shard) * factor
    d_w1, d_w2 = (d_w1 * factor).T, d_w2 * factor
    return (d_input.reshape(block_input.shape), d_w1, d_b1, d_w2, param_grads)


def solution(mesh):
    fine = Mesh(mesh.devices.reshape(SIZES), AXES)
    placed = (
        P(DP, ROWS, None, None),
        P(DP, ROWS, None, None),
        P(),
        P(),
        P(),
        P(),
        P(None, DP),
        P(DP),
        P(DP, None),
        P(),
        P(),
    )
    return jax.shard_map(
        shards,
        mesh=fine,
        in_specs=placed,
        out_specs=(P(DP, ROWS, None, None), P(None, DP), P(DP), P(DP, None), P()),
        check_vma=False,
    )
```

```python
import math

import jax
import jax.numpy as jnp
import numpy as np
from jax import lax
from jax.experimental import pallas as pl
from jax.experimental.pallas import tpu as pltpu
from jax.sharding import Mesh, PartitionSpec as P

KERNEL = 7
MARGIN = 3
EPSILON = 1e-06
INV_ROOT_TWO = 0.7071067811865476
INV_ROOT_TWO_PI = 0.3989422804014327

AXES = ("y_lo", "z", "core", "y_hi", "x")
SIZES = (2, 8, 2, 2, 4)
DP = ("y_lo", "z", "core")
ROWS = ("y_hi", "x")
PAIRS = ("y_lo", "z")
Y = ("y_lo", "y_hi")


def halo(cells):
    down = [(i, i + 1) for i in range(7)]
    up = [(i + 1, i) for i in range(7)]
    above = lax.ppermute(cells[:, -MARGIN:], ROWS, down)
    below = lax.ppermute(cells[:, :MARGIN], ROWS, up)
    return jnp.concatenate([above, cells, below], axis=1)


def swap(cells):
    return lax.ppermute(cells, "core", [(0, 1), (1, 0)])


def spread_sum(part, axes):
    count = lax.axis_size(axes)
    pieces = part.reshape((count, part.shape[0] // count) + part.shape[1:])
    pieces = lax.all_to_all(pieces, axes, 0, 0)
    return jnp.sum(pieces.astype(jnp.float32), axis=0)


def gather(part, axes):
    count = lax.axis_size(axes)
    return lax.all_to_all(jnp.broadcast_to(part[None], (count,) + part.shape), axes, 0, 0)


def across(cells, m):
    flip = (m % 2) * 2 + m // 2
    return lax.ppermute(cells, Y, [(i, i ^ flip) for i in range(4)])


def gather_weights(w1_t, w2, b1):
    whole = lax.all_gather(jnp.concatenate([w1_t, w2], axis=1), PAIRS, axis=0, tiled=True)
    bias = gather(b1.astype(jnp.float32), PAIRS).reshape(-1)
    return whole, bias


def scatter_terms(first, parts):
    own, near, far, last = parts
    half = far.shape[0] // 2
    up = across(far[:half], 1).astype(jnp.float32)
    down = across(far[half:], 3).astype(jnp.float32)
    last = jnp.concatenate(
        [(last[:half].astype(jnp.float32) + up).astype(jnp.bfloat16), last[half:]], axis=0
    )
    near = jnp.concatenate(
        [near[:half], (near[half:].astype(jnp.float32) + down).astype(jnp.bfloat16)], axis=0
    )
    second = own.astype(jnp.float32)
    second = second + across(near, 1).astype(jnp.float32) + across(last, 3).astype(jnp.float32)
    first = jnp.sum(lax.all_to_all(first, "x", 0, 0).astype(jnp.float32), axis=0)
    first = first.astype(jnp.bfloat16).reshape(2, 4, 2, 48, 384)
    first, second = lax.optimization_barrier((first, second.astype(jnp.bfloat16)))
    second = spread_sum(second, "x")
    y_lo, y_hi = lax.axis_index("y_lo"), lax.axis_index("y_hi")
    sent = [
        lax.dynamic_slice(
            first, (y_lo ^ (m % 2), 0, y_hi ^ (m // 2), 0, 0), (1, 4, 1, 48, 384)
        ).reshape(192, 384)
        for m in range(4)
    ]
    first = sent[0].astype(jnp.float32)
    for m in (1, 2, 3):
        first = first + across(sent[m], m).astype(jnp.float32)
    return first, second


def two(cells):
    high = lax.reduce_precision(cells, 8, 7)
    return jnp.concatenate([high, cells - high], axis=0).astype(jnp.bfloat16)


def finish(first, second, small):
    small = small + swap(small)
    small = small + lax.ppermute(small, "y_lo", [(0, 1), (1, 0)])
    first, second, small = lax.optimization_barrier((first, second, small))
    small = spread_sum(small, ROWS)
    small = two(jnp.concatenate([small[:, :384], small[:, 384:]], axis=0))
    terms = jnp.concatenate([first, second], axis=0).astype(jnp.bfloat16).reshape(8, 48, 384)
    small = jnp.broadcast_to(small[None], (8,) + small.shape)
    pieces = lax.all_to_all(jnp.concatenate([terms, small], axis=1), "z", 0, 0)
    total = jnp.sum(pieces.astype(jnp.float32), axis=0)
    small = two(total[48:64] + total[64:])
    total = gather(jnp.concatenate([total[:48].astype(jnp.bfloat16), small], axis=0), ROWS)
    total = total.astype(jnp.float32)
    share = total[:, :48].reshape(2, 4, 48, 384).transpose(0, 2, 1, 3).reshape(96, 1536)
    small = (total[:, 48:64] + total[:, 64:]).reshape(8, 2, 8, 384).transpose(0, 2, 1, 3)
    return share, small.reshape(-1, 768)


BLOCK = 384
LANES = 128
NT = (((1,), (1,)), ((), ()))
NN = (((1,), (0,)), ((), ()))
TN = (((0,), (0,)), ((), ()))
VMEM = 56 * 2**20


def mlp_kernel(
    place, normed, scaled, w1, w2, b1, first, m0, m1, m2, m3, own, peer, d_b1, row, sums
):
    @pl.when(pl.program_id(0) == 0)
    def _():
        sums[...] = jnp.zeros_like(sums)
        row[...] = jnp.zeros_like(row)

    n, s = normed[...], scaled[...]
    step = pl.program_id(0)
    preact = lax.dot_general(w1[...], n, NT, preferred_element_type=jnp.float32) + b1[:, :1]
    cdf = 0.5 * (1.0 + lax.erf(preact * INV_ROOT_TWO))
    hidden = (preact * cdf).astype(jnp.bfloat16)
    slope = cdf + preact * jnp.exp(-0.5 * preact * preact) * INV_ROOT_TWO_PI
    grad_hidden = lax.dot_general(w2[...], s, NT, preferred_element_type=jnp.float32)
    grad_preact = (grad_hidden * slope).astype(jnp.bfloat16)
    moment = lax.dot_general(hidden, s, NN, preferred_element_type=jnp.float32)
    d_w1 = lax.dot_general(grad_preact, n, NN, preferred_element_type=jnp.float32)
    quarters = [
        half[:, at : at + 384].astype(jnp.bfloat16) for half in (d_w1, moment) for at in (0, 384)
    ]

    for y_lo in range(2):

        @pl.when(step == 2 * y_lo)
        def _():
            for x in range(4):
                first[x, y_lo * BLOCK : (y_lo + 1) * BLOCK] = quarters[x]

    for y_hi in range(2):
        m = ((step // 2) ^ place[0]) + 2 * (y_hi ^ place[1])
        for k, part in enumerate((m0, m1, m2, m3)):

            @pl.when((step % 2 == 1) & (m == k))
            def _():
                for x in range(4):
                    for z in range(4):
                        at = x * 192 + z * 48
                        rows = quarters[x][z * 96 + y_hi * 48 : z * 96 + y_hi * 48 + 48]
                        part[at : at + 48] = rows

    row[...] += jnp.sum(moment * w2[...].astype(jnp.float32), axis=0, keepdims=True)
    d_b1[...] = jnp.broadcast_to(
        jnp.sum(grad_preact.astype(jnp.float32), axis=1, keepdims=True), d_b1.shape
    )
    sums[...] += lax.dot_general(grad_preact, w1[...], TN, preferred_element_type=jnp.float32)

    @pl.when(pl.program_id(0) == pl.num_programs(0) - 1)
    def _():
        half = own.shape[0]
        own[...] = sums[:half]
        peer[...] = sums[half:].astype(jnp.bfloat16)


def mlp(normed, scaled, weights, b1):
    pixels, chans = normed.shape
    hid = weights.shape[0]
    place = jnp.stack([lax.axis_index("y_lo"), lax.axis_index("y_hi")]).astype(jnp.int32)
    whole = pl.BlockSpec((pixels, chans), lambda i: (0, 0))
    half = pl.BlockSpec((pixels // 2, chans), lambda i: (0, 0))
    part = pl.BlockSpec((hid // 2, chans // 2), lambda i: (0, 0))
    lane = pl.BlockSpec((BLOCK, LANES), lambda i: (i, 0))
    return pl.pallas_call(
        mlp_kernel,
        grid=(hid // BLOCK,),
        in_specs=[
            pl.BlockSpec(memory_space=pltpu.SMEM),
            whole,
            whole,
            pl.BlockSpec((BLOCK, chans), lambda i: (i, 0)),
            pl.BlockSpec((BLOCK, chans), lambda i: (i, 1)),
            lane,
        ],
        out_specs=[
            pl.BlockSpec((4, hid // 2, chans // 2), lambda i: (0, 0, 0)),
            part,
            part,
            part,
            part,
            half,
            half,
            lane,
            pl.BlockSpec((1, chans), lambda i: (0, 0)),
        ],
        out_shape=[jax.ShapeDtypeStruct((4, hid // 2, chans // 2), jnp.bfloat16)]
        + [jax.ShapeDtypeStruct((hid // 2, chans // 2), jnp.bfloat16)] * 4
        + [
            jax.ShapeDtypeStruct((pixels // 2, chans), jnp.float32),
            jax.ShapeDtypeStruct((pixels // 2, chans), jnp.bfloat16),
            jax.ShapeDtypeStruct((hid, LANES), jnp.float32),
            jax.ShapeDtypeStruct((1, chans), jnp.float32),
        ],
        scratch_shapes=[pltpu.VMEM((pixels, chans), jnp.float32)],
        compiler_params=pltpu.CompilerParams(vmem_limit_bytes=VMEM),
        cost_estimate=pl.CostEstimate(
            flops=10 * pixels * hid * chans, bytes_accessed=2**24, transcendentals=2 * pixels * hid
        ),
    )(place, normed, scaled, weights, weights, jnp.broadcast_to(b1[:, None], (hid, LANES)))


def transposed_kernel(padded, cotangent, kernel, d_input, wide):
    rows, cols = d_input.shape[1:3]
    wide[...] = padded[0].astype(jnp.float32)
    for at in range(0, cols, 24):
        sums = [cotangent[0, r, at : at + 24].astype(jnp.float32) for r in range(rows)]
        for b in range(KERNEL):
            column = [(KERNEL - 1 - a) * KERNEL + KERNEL - 1 - b for a in range(KERNEL)]
            taps = [kernel[t : t + 1] for t in column]
            for r in range(rows + KERNEL - 1):
                cells = wide[r, at + b : at + b + 24]
                for a in range(max(0, r - rows + 1), min(KERNEL, r + 1)):
                    sums[r - a] = sums[r - a] + cells * taps[a]
        for r in range(rows):
            d_input[0, r, at : at + 24] = sums[r].astype(jnp.bfloat16)


def transposed(padded, cotangent, kernel):
    images, high, wide, chans = padded.shape
    rows, cols = cotangent.shape[1:3]
    maps = pl.BlockSpec((1, rows, cols, LANES), lambda c, i: (i, 0, 0, c))
    return pl.pallas_call(
        transposed_kernel,
        grid=(chans // LANES, images),
        in_specs=[
            pl.BlockSpec((1, high, wide, LANES), lambda c, i: (i, 0, 0, c)),
            maps,
            pl.BlockSpec((KERNEL * KERNEL, LANES), lambda c, i: (0, c)),
        ],
        out_specs=maps,
        out_shape=jax.ShapeDtypeStruct(cotangent.shape, jnp.bfloat16),
        scratch_shapes=[pltpu.VMEM((high, wide, LANES), jnp.float32)],
        compiler_params=pltpu.CompilerParams(vmem_limit_bytes=VMEM),
        cost_estimate=pl.CostEstimate(
            flops=10**10, bytes_accessed=2**22, transcendentals=0
        ),
    )(padded, cotangent, kernel)


def taps_kernel(padded, grad, sums, wide, grad_wide):
    rows, cols = grad.shape[1:3]
    wide[...] = padded[0].astype(jnp.float32)
    grad_wide[...] = grad[0].astype(jnp.float32)

    @pl.when(pl.program_id(1) == 0)
    def _():
        sums[...] = jnp.zeros_like(sums)

    for b in range(KERNEL):
        totals = [jnp.zeros((8, LANES), jnp.float32) for _ in range(KERNEL)]
        for at in range(0, cols, 16):
            own = [grad_wide[r, at : at + 16] for r in range(rows)]
            for r in range(rows + KERNEL - 1):
                cells = wide[r, at + b : at + b + 16]
                for a in range(max(0, r - rows + 1), min(KERNEL, r + 1)):
                    product = cells * own[r - a]
                    totals[a] = totals[a] + (product[:8] + product[8:])
        for a in range(KERNEL):
            t = a * KERNEL + b
            sums[t : t + 1] += jnp.sum(totals[a], axis=0, keepdims=True)


def tap_sums(padded, grad):
    images, high, wide, chans = padded.shape
    rows, cols = grad.shape[1:3]
    return pl.pallas_call(
        taps_kernel,
        grid=(chans // LANES, images),
        in_specs=[
            pl.BlockSpec((1, high, wide, LANES), lambda c, i: (i, 0, 0, c)),
            pl.BlockSpec((1, rows, cols, LANES), lambda c, i: (i, 0, 0, c)),
        ],
        out_specs=pl.BlockSpec((KERNEL * KERNEL, LANES), lambda c, i: (0, c)),
        out_shape=jax.ShapeDtypeStruct((KERNEL * KERNEL, chans), jnp.float32),
        scratch_shapes=[
            pltpu.VMEM((high, wide, LANES), jnp.float32),
            pltpu.VMEM((rows, cols, LANES), jnp.float32),
        ],
        compiler_params=pltpu.CompilerParams(vmem_limit_bytes=VMEM),
        cost_estimate=pl.CostEstimate(
            flops=10**10, bytes_accessed=2**22, transcendentals=0
        ),
    )(padded, grad)


def pad_columns(cells):
    return jnp.pad(cells, ((0, 0), (0, 0), (MARGIN, 8 - MARGIN), (0, 0)))


def depthwise(padded, kernel, height, width):
    total = jnp.zeros(padded.shape[:-3] + (height, width, padded.shape[-1]), jnp.float32)
    for row_tap in range(KERNEL):
        for col_tap in range(KERNEL):
            window = padded[:, row_tap : row_tap + height, col_tap : col_tap + width]
            total = total + window.astype(jnp.float32) * kernel[row_tap * KERNEL + col_tap]
    return total


def shards(block_input, cotangent, dw_kernel, dw_bias, ln_gain, ln_bias, w1, b1, w2, b2, gamma):
    images, rows_here, cols, chans = block_input.shape
    shard = w1.shape[1]
    pixels = images * rows_here * cols
    flat_cot = cotangent.reshape(pixels, chans).astype(jnp.float32)
    scaled = (flat_cot * gamma).astype(jnp.bfloat16)
    weights, b1_h = gather_weights(w1.T, w2, b1)
    padded = pad_columns(halo(block_input))
    scaled2 = jnp.concatenate([scaled, swap(scaled)], axis=0)
    conv = depthwise(padded, dw_kernel, rows_here, cols) + dw_bias
    center = conv - jnp.mean(conv, axis=-1, keepdims=True)
    spread = jnp.mean(center * center, axis=-1, keepdims=True)
    rstd = lax.rsqrt(spread + EPSILON).reshape(pixels, 1)
    norm = center.reshape(pixels, chans) * rstd
    normed = (norm * ln_gain + ln_bias).astype(jnp.bfloat16)
    normed2 = jnp.concatenate([normed, swap(normed)], axis=0)

    first, *parts, own, peer, sums_b1, moment_row = mlp(normed2, scaled2, weights, b1_h)
    first, second = scatter_terms(first, parts)
    grad_normed = own + swap(peer).astype(jnp.float32)

    weighted = grad_normed * ln_gain
    grad_conv = (
        rstd
        * (
            weighted
            - jnp.mean(weighted, axis=-1, keepdims=True)
            - norm * jnp.mean(weighted * norm, axis=-1, keepdims=True)
        )
    ).astype(jnp.bfloat16)
    grad_maps = grad_conv.reshape(block_input.shape)
    grad_padded = pad_columns(halo(grad_maps))
    d_input = transposed(grad_padded, cotangent, dw_kernel)

    grad_wide = grad_maps.astype(jnp.float32)
    cot_sums = jnp.sum(flat_cot, axis=0)
    core = lax.axis_index("core")
    y_lo = lax.axis_index("y_lo")
    sums_b1 = sums_b1[:, 0][None]
    pair_b1 = jnp.where(core == jnp.arange(2)[:, None], sums_b1, 0.0)
    local_small = jnp.concatenate(
        [
            tap_sums(padded, grad_maps),
            jnp.sum(grad_wide, axis=(0, 1, 2))[None],
            jnp.sum(grad_normed * norm, axis=0)[None],
            jnp.sum(grad_normed, axis=0)[None],
            (gamma * cot_sums)[None],
            moment_row / gamma + b2 * cot_sums,
            pair_b1.reshape(-1, chans),
            jnp.zeros((6, chans), jnp.float32),
        ],
        axis=0,
    )
    share, total_small = finish(first, second, local_small)
    factor = 1.0 / math.sqrt(pixels * 256)
    param_grads = total_small[:54] * factor
    at = (y_lo * 8 + lax.axis_index("z")) * shard
    sums = total_small[54:58].reshape(2, -1)
    d_b1 = lax.dynamic_slice(sums, (core, at), (1, shard)).reshape(shard) * factor
    share = share * factor
    d_w1, d_w2 = share[:, :chans].T, share[:, chans:]
    return (d_input.reshape(block_input.shape), d_w1, d_b1, d_w2, param_grads)


def solution(mesh):
    fine = Mesh(mesh.devices.reshape(SIZES), AXES)
    placed = (
        P(DP, ROWS, None, None),
        P(DP, ROWS, None, None),
        P(),
        P(),
        P(),
        P(),
        P(None, DP),
        P(DP),
        P(DP, None),
        P(),
        P(),
    )
    return jax.shard_map(
        shards,
        mesh=fine,
        in_specs=placed,
        out_specs=(P(DP, ROWS, None, None), P(None, DP), P(DP), P(DP, None), P()),
        check_vma=False,
    )
```

```python
import math

import jax
import jax.numpy as jnp
import numpy as np
from jax import lax
from jax.experimental import pallas as pl
from jax.experimental.pallas import tpu as pltpu
from jax.sharding import Mesh, PartitionSpec as P

KERNEL = 7
MARGIN = 3
EPSILON = 1e-06
INV_ROOT_TWO = 0.7071067811865476
INV_ROOT_TWO_PI = 0.3989422804014327

AXES = ("y_lo", "z", "core", "y_hi", "x")
SIZES = (2, 8, 2, 2, 4)
DP = ("y_lo", "z", "core")
ROWS = ("y_hi", "x")
PAIRS = ("y_lo", "z")
Y = ("y_lo", "y_hi")


def halo(cells):
    down = [(i, i + 1) for i in range(7)]
    up = [(i + 1, i) for i in range(7)]
    above = lax.ppermute(cells[:, -MARGIN:], ROWS, down)
    below = lax.ppermute(cells[:, :MARGIN], ROWS, up)
    return jnp.concatenate([above, cells, below], axis=1)


def swap(cells):
    return lax.ppermute(cells, "core", [(0, 1), (1, 0)])


def spread_sum(part, axes):
    count = lax.axis_size(axes)
    pieces = part.reshape((count, part.shape[0] // count) + part.shape[1:])
    pieces = lax.all_to_all(pieces, axes, 0, 0)
    return jnp.sum(pieces.astype(jnp.float32), axis=0)


def gather(part, axes):
    count = lax.axis_size(axes)
    return lax.all_to_all(jnp.broadcast_to(part[None], (count,) + part.shape), axes, 0, 0)


def across(cells, m):
    flip = (m % 2) * 2 + m // 2
    return lax.ppermute(cells, Y, [(i, i ^ flip) for i in range(4)])


def gather_weights(w1_t, w2, b1):
    whole = lax.all_gather(jnp.concatenate([w1_t, w2], axis=1), PAIRS, axis=0, tiled=True)
    bias = gather(b1.astype(jnp.float32), PAIRS).reshape(-1)
    return whole, bias


def scatter_terms(first, parts):
    second = parts[0].astype(jnp.float32)
    for m in (1, 2, 3):
        second = second + across(parts[m], m).astype(jnp.float32)
    first = jnp.sum(lax.all_to_all(first, "x", 0, 0).astype(jnp.float32), axis=0)
    first = first.astype(jnp.bfloat16).reshape(2, 4, 2, 48, 384)
    first, second = lax.optimization_barrier((first, second.astype(jnp.bfloat16)))
    second = spread_sum(second, "x")
    y_lo, y_hi = lax.axis_index("y_lo"), lax.axis_index("y_hi")
    sent = [
        lax.dynamic_slice(
            first, (y_lo ^ (m % 2), 0, y_hi ^ (m // 2), 0, 0), (1, 4, 1, 48, 384)
        ).reshape(192, 384)
        for m in range(4)
    ]
    first = sent[0].astype(jnp.float32)
    for m in (1, 2, 3):
        first = first + across(sent[m], m).astype(jnp.float32)
    return first, second


def two(cells):
    high = lax.reduce_precision(cells, 8, 7)
    return jnp.concatenate([high, cells - high], axis=0).astype(jnp.bfloat16)


def spread_small(small):
    x, y_hi = lax.axis_index("x"), lax.axis_index("y_hi")
    small = small + swap(small)
    small = small + across(small, 1)
    mine = lax.dynamic_slice(small, (y_hi * 32, 0), (32, 768))
    small = mine + across(lax.dynamic_slice(small, ((1 - y_hi) * 32, 0), (32, 768)), 2)
    total = lax.dynamic_slice(small, (x * 8, 0), (8, 768))
    for k in (1, 2, 3):
        sent = lax.dynamic_slice(small, ((x + k) % 4 * 8, 0), (8, 768))
        total = total + lax.ppermute(sent, "x", [(i, (i + k) % 4) for i in range(4)])
    return total


def finish(first, second, small, beside):
    small = spread_small(small)
    work, cells = beside
    cells, first, second, small = lax.optimization_barrier((cells, first, second, small))
    small = two(jnp.concatenate([small[:, :384], small[:, 384:]], axis=0))
    terms = jnp.concatenate([first, second], axis=0).astype(jnp.bfloat16).reshape(8, 48, 384)
    small = jnp.broadcast_to(small[None], (8,) + small.shape)
    pieces = lax.all_to_all(jnp.concatenate([terms, small], axis=1), "z", 0, 0)
    pieces, done = lax.optimization_barrier((pieces, work(cells)))
    total = jnp.sum(pieces.astype(jnp.float32), axis=0)
    small = two(total[48:64] + total[64:])
    total = gather(jnp.concatenate([total[:48].astype(jnp.bfloat16), small], axis=0), ROWS)
    total = total.astype(jnp.float32)
    share = total[:, :48].reshape(2, 4, 48, 384).transpose(0, 2, 1, 3).reshape(96, 1536)
    small = (total[:, 48:64] + total[:, 64:]).reshape(8, 2, 8, 384).transpose(0, 2, 1, 3)
    return share, small.reshape(-1, 768), done


BLOCK = 384
LANES = 128
NT = (((1,), (1,)), ((), ()))
NN = (((1,), (0,)), ((), ()))
TN = (((0,), (0,)), ((), ()))
VMEM = 56 * 2**20


def mlp_kernel(
    place, normed, scaled, w1, w2, b1, first, m0, m1, m2, m3, own, peer, d_b1, row, sums
):
    @pl.when(pl.program_id(0) == 0)
    def _():
        sums[...] = jnp.zeros_like(sums)
        row[...] = jnp.zeros_like(row)

    n, s = normed[...], scaled[...]
    step = pl.program_id(0)
    preact = lax.dot_general(w1[...], n, NT, preferred_element_type=jnp.float32) + b1[:, :1]
    cdf = 0.5 * (1.0 + lax.erf(preact * INV_ROOT_TWO))
    hidden = (preact * cdf).astype(jnp.bfloat16)
    slope = cdf + preact * jnp.exp(-0.5 * preact * preact) * INV_ROOT_TWO_PI
    grad_hidden = lax.dot_general(w2[...], s, NT, preferred_element_type=jnp.float32)
    grad_preact = (grad_hidden * slope).astype(jnp.bfloat16)
    moment = lax.dot_general(hidden, s, NN, preferred_element_type=jnp.float32)
    d_w1 = lax.dot_general(grad_preact, n, NN, preferred_element_type=jnp.float32)
    quarters = [
        half[:, at : at + 384].astype(jnp.bfloat16) for half in (d_w1, moment) for at in (0, 384)
    ]

    for y_lo in range(2):

        @pl.when(step == 2 * y_lo)
        def _():
            for x in range(4):
                first[x, y_lo * BLOCK : (y_lo + 1) * BLOCK] = quarters[x]

    for y_hi in range(2):
        m = ((step // 2) ^ place[0]) + 2 * (y_hi ^ place[1])
        for k, part in enumerate((m0, m1, m2, m3)):

            @pl.when((step % 2 == 1) & (m == k))
            def _():
                for x in range(4):
                    for z in range(4):
                        at = x * 192 + z * 48
                        rows = quarters[x][z * 96 + y_hi * 48 : z * 96 + y_hi * 48 + 48]
                        part[at : at + 48] = rows

    row[...] += jnp.sum(moment * w2[...].astype(jnp.float32), axis=0, keepdims=True)
    d_b1[...] = jnp.broadcast_to(
        jnp.sum(grad_preact.astype(jnp.float32), axis=1, keepdims=True), d_b1.shape
    )
    sums[...] += lax.dot_general(grad_preact, w1[...], TN, preferred_element_type=jnp.float32)

    @pl.when(pl.program_id(0) == pl.num_programs(0) - 1)
    def _():
        half = own.shape[0]
        own[...] = sums[:half]
        peer[...] = sums[half:].astype(jnp.bfloat16)


def mlp(normed, scaled, weights, b1):
    pixels, chans = normed.shape
    hid = weights.shape[0]
    place = jnp.stack([lax.axis_index("y_lo"), lax.axis_index("y_hi")]).astype(jnp.int32)
    whole = pl.BlockSpec((pixels, chans), lambda i: (0, 0))
    half = pl.BlockSpec((pixels // 2, chans), lambda i: (0, 0))
    part = pl.BlockSpec((hid // 2, chans // 2), lambda i: (0, 0))
    lane = pl.BlockSpec((BLOCK, LANES), lambda i: (i, 0))
    return pl.pallas_call(
        mlp_kernel,
        grid=(hid // BLOCK,),
        in_specs=[
            pl.BlockSpec(memory_space=pltpu.SMEM),
            whole,
            whole,
            pl.BlockSpec((BLOCK, chans), lambda i: (i, 0)),
            pl.BlockSpec((BLOCK, chans), lambda i: (i, 1)),
            lane,
        ],
        out_specs=[
            pl.BlockSpec((4, hid // 2, chans // 2), lambda i: (0, 0, 0)),
            part,
            part,
            part,
            part,
            half,
            half,
            lane,
            pl.BlockSpec((1, chans), lambda i: (0, 0)),
        ],
        out_shape=[jax.ShapeDtypeStruct((4, hid // 2, chans // 2), jnp.bfloat16)]
        + [jax.ShapeDtypeStruct((hid // 2, chans // 2), jnp.bfloat16)] * 4
        + [
            jax.ShapeDtypeStruct((pixels // 2, chans), jnp.float32),
            jax.ShapeDtypeStruct((pixels // 2, chans), jnp.bfloat16),
            jax.ShapeDtypeStruct((hid, LANES), jnp.float32),
            jax.ShapeDtypeStruct((1, chans), jnp.float32),
        ],
        scratch_shapes=[pltpu.VMEM((pixels, chans), jnp.float32)],
        compiler_params=pltpu.CompilerParams(vmem_limit_bytes=VMEM),
        cost_estimate=pl.CostEstimate(
            flops=10 * pixels * hid * chans, bytes_accessed=2**24, transcendentals=2 * pixels * hid
        ),
    )(place, normed, scaled, weights, weights, jnp.broadcast_to(b1[:, None], (hid, LANES)))


def transposed_kernel(padded, cotangent, kernel, d_input, wide):
    rows, cols = d_input.shape[1:3]
    wide[...] = padded[0].astype(jnp.float32)
    for at in range(0, cols, 24):
        sums = [cotangent[0, r, at : at + 24].astype(jnp.float32) for r in range(rows)]
        for b in range(KERNEL):
            column = [(KERNEL - 1 - a) * KERNEL + KERNEL - 1 - b for a in range(KERNEL)]
            taps = [kernel[t : t + 1] for t in column]
            for r in range(rows + KERNEL - 1):
                cells = wide[r, at + b : at + b + 24]
                for a in range(max(0, r - rows + 1), min(KERNEL, r + 1)):
                    sums[r - a] = sums[r - a] + cells * taps[a]
        for r in range(rows):
            d_input[0, r, at : at + 24] = sums[r].astype(jnp.bfloat16)


def transposed(padded, cotangent, kernel):
    images, high, wide, chans = padded.shape
    rows, cols = cotangent.shape[1:3]
    maps = pl.BlockSpec((1, rows, cols, LANES), lambda c, i: (i, 0, 0, c))
    return pl.pallas_call(
        transposed_kernel,
        grid=(chans // LANES, images),
        in_specs=[
            pl.BlockSpec((1, high, wide, LANES), lambda c, i: (i, 0, 0, c)),
            maps,
            pl.BlockSpec((KERNEL * KERNEL, LANES), lambda c, i: (0, c)),
        ],
        out_specs=maps,
        out_shape=jax.ShapeDtypeStruct(cotangent.shape, jnp.bfloat16),
        scratch_shapes=[pltpu.VMEM((high, wide, LANES), jnp.float32)],
        compiler_params=pltpu.CompilerParams(vmem_limit_bytes=VMEM),
        cost_estimate=pl.CostEstimate(
            flops=10**10, bytes_accessed=2**22, transcendentals=0
        ),
    )(padded, cotangent, kernel)


def taps_kernel(padded, grad, sums, wide, grad_wide):
    rows, cols = grad.shape[1:3]
    wide[...] = padded[0].astype(jnp.float32)
    grad_wide[...] = grad[0].astype(jnp.float32)

    @pl.when(pl.program_id(1) == 0)
    def _():
        sums[...] = jnp.zeros_like(sums)

    for b in range(KERNEL):
        totals = [jnp.zeros((8, LANES), jnp.float32) for _ in range(KERNEL)]
        for at in range(0, cols, 16):
            own = [grad_wide[r, at : at + 16] for r in range(rows)]
            for r in range(rows + KERNEL - 1):
                cells = wide[r, at + b : at + b + 16]
                for a in range(max(0, r - rows + 1), min(KERNEL, r + 1)):
                    product = cells * own[r - a]
                    totals[a] = totals[a] + (product[:8] + product[8:])
        for a in range(KERNEL):
            t = a * KERNEL + b
            sums[t : t + 1] += jnp.sum(totals[a], axis=0, keepdims=True)


def tap_sums(padded, grad):
    images, high, wide, chans = padded.shape
    rows, cols = grad.shape[1:3]
    return pl.pallas_call(
        taps_kernel,
        grid=(chans // LANES, images),
        in_specs=[
            pl.BlockSpec((1, high, wide, LANES), lambda c, i: (i, 0, 0, c)),
            pl.BlockSpec((1, rows, cols, LANES), lambda c, i: (i, 0, 0, c)),
        ],
        out_specs=pl.BlockSpec((KERNEL * KERNEL, LANES), lambda c, i: (0, c)),
        out_shape=jax.ShapeDtypeStruct((KERNEL * KERNEL, chans), jnp.float32),
        scratch_shapes=[
            pltpu.VMEM((high, wide, LANES), jnp.float32),
            pltpu.VMEM((rows, cols, LANES), jnp.float32),
        ],
        compiler_params=pltpu.CompilerParams(vmem_limit_bytes=VMEM),
        cost_estimate=pl.CostEstimate(
            flops=10**10, bytes_accessed=2**22, transcendentals=0
        ),
    )(padded, grad)


def pad_columns(cells):
    return jnp.pad(cells, ((0, 0), (0, 0), (MARGIN, 8 - MARGIN), (0, 0)))


def depthwise(padded, kernel, height, width):
    total = jnp.zeros(padded.shape[:-3] + (height, width, padded.shape[-1]), jnp.float32)
    for row_tap in range(KERNEL):
        for col_tap in range(KERNEL):
            window = padded[:, row_tap : row_tap + height, col_tap : col_tap + width]
            total = total + window.astype(jnp.float32) * kernel[row_tap * KERNEL + col_tap]
    return total


def shards(block_input, cotangent, dw_kernel, dw_bias, ln_gain, ln_bias, w1, b1, w2, b2, gamma):
    images, rows_here, cols, chans = block_input.shape
    shard = w1.shape[1]
    pixels = images * rows_here * cols
    flat_cot = cotangent.reshape(pixels, chans).astype(jnp.float32)
    scaled = (flat_cot * gamma).astype(jnp.bfloat16)
    weights, b1_h = gather_weights(w1.T, w2, b1)
    padded = pad_columns(halo(block_input))
    scaled2 = jnp.concatenate([scaled, swap(scaled)], axis=0)
    conv = depthwise(padded, dw_kernel, rows_here, cols) + dw_bias
    center = conv - jnp.mean(conv, axis=-1, keepdims=True)
    spread = jnp.mean(center * center, axis=-1, keepdims=True)
    rstd = lax.rsqrt(spread + EPSILON).reshape(pixels, 1)
    norm = center.reshape(pixels, chans) * rstd
    normed = (norm * ln_gain + ln_bias).astype(jnp.bfloat16)
    normed2 = jnp.concatenate([normed, swap(normed)], axis=0)

    first, *parts, own, peer, sums_b1, moment_row = mlp(normed2, scaled2, weights, b1_h)
    first, second = scatter_terms(first, parts)
    grad_normed = own + swap(peer).astype(jnp.float32)

    weighted = grad_normed * ln_gain
    grad_conv = (
        rstd
        * (
            weighted
            - jnp.mean(weighted, axis=-1, keepdims=True)
            - norm * jnp.mean(weighted * norm, axis=-1, keepdims=True)
        )
    ).astype(jnp.bfloat16)
    grad_maps = grad_conv.reshape(block_input.shape)
    grad_padded = pad_columns(halo(grad_maps))

    grad_wide = grad_maps.astype(jnp.float32)
    cot_sums = jnp.sum(flat_cot, axis=0)
    core = lax.axis_index("core")
    y_lo = lax.axis_index("y_lo")
    sums_b1 = sums_b1[:, 0][None]
    pair_b1 = jnp.where(core == jnp.arange(2)[:, None], sums_b1, 0.0)
    local_small = jnp.concatenate(
        [
            tap_sums(padded, grad_maps),
            jnp.sum(grad_wide, axis=(0, 1, 2))[None],
            jnp.sum(grad_normed * norm, axis=0)[None],
            jnp.sum(grad_normed, axis=0)[None],
            (gamma * cot_sums)[None],
            moment_row / gamma + b2 * cot_sums,
            pair_b1.reshape(-1, chans),
            jnp.zeros((6, chans), jnp.float32),
        ],
        axis=0,
    )
    share, total_small, d_input = finish(
        first, second, local_small, (lambda g: transposed(g, cotangent, dw_kernel), grad_padded)
    )
    factor = 1.0 / math.sqrt(pixels * 256)
    param_grads = total_small[:54] * factor
    at = (y_lo * 8 + lax.axis_index("z")) * shard
    sums = total_small[54:58].reshape(2, -1)
    d_b1 = lax.dynamic_slice(sums, (core, at), (1, shard)).reshape(shard) * factor
    share = share * factor
    d_w1, d_w2 = share[:, :chans].T, share[:, chans:]
    return (d_input.reshape(block_input.shape), d_w1, d_b1, d_w2, param_grads)


def solution(mesh):
    fine = Mesh(mesh.devices.reshape(SIZES), AXES)
    placed = (
        P(DP, ROWS, None, None),
        P(DP, ROWS, None, None),
        P(),
        P(),
        P(),
        P(),
        P(None, DP),
        P(DP),
        P(DP, None),
        P(),
        P(),
    )
    return jax.shard_map(
        shards,
        mesh=fine,
        in_specs=placed,
        out_specs=(P(DP, ROWS, None, None), P(None, DP), P(DP), P(DP, None), P()),
        check_vma=False,
    )
```

```python
import math

import jax
import jax.numpy as jnp
import numpy as np
from jax import lax
from jax.experimental import pallas as pl
from jax.experimental.pallas import tpu as pltpu
from jax.sharding import Mesh, PartitionSpec as P

KERNEL = 7
MARGIN = 3
EPSILON = 1e-06
INV_ROOT_TWO = 0.7071067811865476
INV_ROOT_TWO_PI = 0.3989422804014327

AXES = ("y_lo", "z", "core", "y_hi", "x")
SIZES = (2, 8, 2, 2, 4)
DP = ("y_lo", "z", "core")
ROWS = ("y_hi", "x")
PAIRS = ("y_lo", "z")
Y = ("y_lo", "y_hi")


def halo(cells):
    down = [(i, i + 1) for i in range(7)]
    up = [(i + 1, i) for i in range(7)]
    above = lax.ppermute(cells[:, -MARGIN:], ROWS, down)
    below = lax.ppermute(cells[:, :MARGIN], ROWS, up)
    return jnp.concatenate([above, cells, below], axis=1)


def swap(cells):
    return lax.ppermute(cells, "core", [(0, 1), (1, 0)])


def spread_sum(part, axes):
    count = lax.axis_size(axes)
    pieces = part.reshape((count, part.shape[0] // count) + part.shape[1:])
    pieces = lax.all_to_all(pieces, axes, 0, 0)
    return jnp.sum(pieces.astype(jnp.float32), axis=0)


def gather(part, axes):
    count = lax.axis_size(axes)
    return lax.all_to_all(jnp.broadcast_to(part[None], (count,) + part.shape), axes, 0, 0)


def across(cells, m):
    flip = (m % 2) * 2 + m // 2
    return lax.ppermute(cells, Y, [(i, i ^ flip) for i in range(4)])


def gather_weights(w1_t, w2, b1):
    whole = lax.all_gather(jnp.concatenate([w1_t, w2], axis=1), PAIRS, axis=0, tiled=True)
    bias = gather(b1.astype(jnp.float32), PAIRS).reshape(-1)
    return whole, bias


def scatter_terms(first, parts, small):
    second = parts[0].astype(jnp.float32)
    for m in (1, 2, 3):
        second = second + across(parts[m], m).astype(jnp.float32)
    first = jnp.sum(lax.all_to_all(first, "x", 0, 0).astype(jnp.float32), axis=0)
    first = first.astype(jnp.bfloat16).reshape(2, 4, 2, 48, 384)
    small = small + swap(small)
    first, second, small = lax.optimization_barrier((first, second.astype(jnp.bfloat16), small))
    second = spread_sum(second, "x")
    y_lo, y_hi = lax.axis_index("y_lo"), lax.axis_index("y_hi")
    sent = [
        lax.dynamic_slice(
            first, (y_lo ^ (m % 2), 0, y_hi ^ (m // 2), 0, 0), (1, 4, 1, 48, 384)
        ).reshape(192, 384)
        for m in range(4)
    ]
    first = sent[0].astype(jnp.float32)
    for m in (1, 2, 3):
        first = first + across(sent[m], m).astype(jnp.float32)
    return first, second, small


def two(cells):
    high = lax.reduce_precision(cells, 8, 7)
    return jnp.concatenate([high, cells - high], axis=0).astype(jnp.bfloat16)


def spread_small(small):
    x, y_hi = lax.axis_index("x"), lax.axis_index("y_hi")
    mine = lax.dynamic_slice(small, (y_hi * 32, 0), (32, 768))
    other = lax.dynamic_slice(small, ((1 - y_hi) * 32, 0), (32, 768))
    small = mine + across(mine, 1) + across(other, 2) + across(other, 3)
    total = lax.dynamic_slice(small, (x * 8, 0), (8, 768))
    for k in (1, 2, 3):
        sent = lax.dynamic_slice(small, ((x + k) % 4 * 8, 0), (8, 768))
        total = total + lax.ppermute(sent, "x", [(i, (i + k) % 4) for i in range(4)])
    return total


def finish(first, second, small, beside):
    small = spread_small(small)
    work, cells = beside
    cells, first, second, small = lax.optimization_barrier((cells, first, second, small))
    small = two(jnp.concatenate([small[:, :384], small[:, 384:]], axis=0))
    terms = jnp.concatenate([first, second], axis=0).astype(jnp.bfloat16).reshape(8, 48, 384)
    small = jnp.broadcast_to(small[None], (8,) + small.shape)
    pieces = lax.all_to_all(jnp.concatenate([terms, small], axis=1), "z", 0, 0)
    pieces, done = lax.optimization_barrier((pieces, work(cells)))
    total = jnp.sum(pieces.astype(jnp.float32), axis=0)
    small = two(total[48:64] + total[64:])
    total = gather(jnp.concatenate([total[:48].astype(jnp.bfloat16), small], axis=0), ROWS)
    total = total.astype(jnp.float32)
    share = total[:, :48].reshape(2, 4, 48, 384).transpose(0, 2, 1, 3).reshape(96, 1536)
    small = (total[:, 48:64] + total[:, 64:]).reshape(8, 2, 8, 384).transpose(0, 2, 1, 3)
    return share, small.reshape(-1, 768), done


BLOCK = 384
LANES = 128
NT = (((1,), (1,)), ((), ()))
NN = (((1,), (0,)), ((), ()))
TN = (((0,), (0,)), ((), ()))
VMEM = 56 * 2**20


def mlp_kernel(
    place, normed, scaled, w1, w2, b1, first, m0, m1, m2, m3, own, peer, d_b1, row, sums
):
    @pl.when(pl.program_id(0) == 0)
    def _():
        sums[...] = jnp.zeros_like(sums)
        row[...] = jnp.zeros_like(row)

    n, s = normed[...], scaled[...]
    step = pl.program_id(0)
    preact = lax.dot_general(w1[...], n, NT, preferred_element_type=jnp.float32) + b1[:, :1]
    cdf = 0.5 * (1.0 + lax.erf(preact * INV_ROOT_TWO))
    hidden = (preact * cdf).astype(jnp.bfloat16)
    slope = cdf + preact * jnp.exp(-0.5 * preact * preact) * INV_ROOT_TWO_PI
    grad_hidden = lax.dot_general(w2[...], s, NT, preferred_element_type=jnp.float32)
    grad_preact = (grad_hidden * slope).astype(jnp.bfloat16)
    moment = lax.dot_general(hidden, s, NN, preferred_element_type=jnp.float32)
    d_w1 = lax.dot_general(grad_preact, n, NN, preferred_element_type=jnp.float32)
    quarters = [
        half[:, at : at + 384].astype(jnp.bfloat16) for half in (d_w1, moment) for at in (0, 384)
    ]

    for y_lo in range(2):

        @pl.when(step == 2 * y_lo)
        def _():
            for x in range(4):
                first[x, y_lo * BLOCK : (y_lo + 1) * BLOCK] = quarters[x]

    for y_hi in range(2):
        m = ((step // 2) ^ place[0]) + 2 * (y_hi ^ place[1])
        for k, part in enumerate((m0, m1, m2, m3)):

            @pl.when((step % 2 == 1) & (m == k))
            def _():
                for x in range(4):
                    for z in range(4):
                        at = x * 192 + z * 48
                        rows = quarters[x][z * 96 + y_hi * 48 : z * 96 + y_hi * 48 + 48]
                        part[at : at + 48] = rows

    row[...] += jnp.sum(moment * w2[...].astype(jnp.float32), axis=0, keepdims=True)
    d_b1[...] = jnp.broadcast_to(
        jnp.sum(grad_preact.astype(jnp.float32), axis=1, keepdims=True), d_b1.shape
    )
    sums[...] += lax.dot_general(grad_preact, w1[...], TN, preferred_element_type=jnp.float32)

    @pl.when(pl.program_id(0) == pl.num_programs(0) - 1)
    def _():
        half = own.shape[0]
        own[...] = sums[:half]
        peer[...] = sums[half:].astype(jnp.bfloat16)


def mlp(normed, scaled, weights, b1):
    pixels, chans = normed.shape
    hid = weights.shape[0]
    place = jnp.stack([lax.axis_index("y_lo"), lax.axis_index("y_hi")]).astype(jnp.int32)
    whole = pl.BlockSpec((pixels, chans), lambda i: (0, 0))
    half = pl.BlockSpec((pixels // 2, chans), lambda i: (0, 0))
    part = pl.BlockSpec((hid // 2, chans // 2), lambda i: (0, 0))
    lane = pl.BlockSpec((BLOCK, LANES), lambda i: (i, 0))
    return pl.pallas_call(
        mlp_kernel,
        grid=(hid // BLOCK,),
        in_specs=[
            pl.BlockSpec(memory_space=pltpu.SMEM),
            whole,
            whole,
            pl.BlockSpec((BLOCK, chans), lambda i: (i, 0)),
            pl.BlockSpec((BLOCK, chans), lambda i: (i, 1)),
            lane,
        ],
        out_specs=[
            pl.BlockSpec((4, hid // 2, chans // 2), lambda i: (0, 0, 0)),
            part,
            part,
            part,
            part,
            half,
            half,
            lane,
            pl.BlockSpec((1, chans), lambda i: (0, 0)),
        ],
        out_shape=[jax.ShapeDtypeStruct((4, hid // 2, chans // 2), jnp.bfloat16)]
        + [jax.ShapeDtypeStruct((hid // 2, chans // 2), jnp.bfloat16)] * 4
        + [
            jax.ShapeDtypeStruct((pixels // 2, chans), jnp.float32),
            jax.ShapeDtypeStruct((pixels // 2, chans), jnp.bfloat16),
            jax.ShapeDtypeStruct((hid, LANES), jnp.float32),
            jax.ShapeDtypeStruct((1, chans), jnp.float32),
        ],
        scratch_shapes=[pltpu.VMEM((pixels, chans), jnp.float32)],
        compiler_params=pltpu.CompilerParams(vmem_limit_bytes=VMEM),
        cost_estimate=pl.CostEstimate(
            flops=10 * pixels * hid * chans, bytes_accessed=2**24, transcendentals=2 * pixels * hid
        ),
    )(place, normed, scaled, weights, weights, jnp.broadcast_to(b1[:, None], (hid, LANES)))


def transposed_kernel(padded, cotangent, kernel, d_input, wide):
    rows, cols = d_input.shape[1:3]
    wide[...] = padded[0].astype(jnp.float32)
    for at in range(0, cols, 24):
        sums = [cotangent[0, r, at : at + 24].astype(jnp.float32) for r in range(rows)]
        for b in range(KERNEL):
            column = [(KERNEL - 1 - a) * KERNEL + KERNEL - 1 - b for a in range(KERNEL)]
            taps = [kernel[t : t + 1] for t in column]
            for r in range(rows + KERNEL - 1):
                cells = wide[r, at + b : at + b + 24]
                for a in range(max(0, r - rows + 1), min(KERNEL, r + 1)):
                    sums[r - a] = sums[r - a] + cells * taps[a]
        for r in range(rows):
            d_input[0, r, at : at + 24] = sums[r].astype(jnp.bfloat16)


def transposed(padded, cotangent, kernel):
    images, high, wide, chans = padded.shape
    rows, cols = cotangent.shape[1:3]
    maps = pl.BlockSpec((1, rows, cols, LANES), lambda c, i: (i, 0, 0, c))
    return pl.pallas_call(
        transposed_kernel,
        grid=(chans // LANES, images),
        in_specs=[
            pl.BlockSpec((1, high, wide, LANES), lambda c, i: (i, 0, 0, c)),
            maps,
            pl.BlockSpec((KERNEL * KERNEL, LANES), lambda c, i: (0, c)),
        ],
        out_specs=maps,
        out_shape=jax.ShapeDtypeStruct(cotangent.shape, jnp.bfloat16),
        scratch_shapes=[pltpu.VMEM((high, wide, LANES), jnp.float32)],
        compiler_params=pltpu.CompilerParams(vmem_limit_bytes=VMEM),
        cost_estimate=pl.CostEstimate(
            flops=10**10, bytes_accessed=2**22, transcendentals=0
        ),
    )(padded, cotangent, kernel)


def taps_kernel(padded, grad, sums, wide, grad_wide):
    rows, cols = grad.shape[1:3]
    wide[...] = padded[0].astype(jnp.float32)
    grad_wide[...] = grad[0].astype(jnp.float32)

    @pl.when(pl.program_id(1) == 0)
    def _():
        sums[...] = jnp.zeros_like(sums)

    for b in range(KERNEL):
        totals = [jnp.zeros((8, LANES), jnp.float32) for _ in range(KERNEL)]
        for at in range(0, cols, 16):
            own = [grad_wide[r, at : at + 16] for r in range(rows)]
            for r in range(rows + KERNEL - 1):
                cells = wide[r, at + b : at + b + 16]
                for a in range(max(0, r - rows + 1), min(KERNEL, r + 1)):
                    product = cells * own[r - a]
                    totals[a] = totals[a] + (product[:8] + product[8:])
        for a in range(KERNEL):
            t = a * KERNEL + b
            sums[t : t + 1] += jnp.sum(totals[a], axis=0, keepdims=True)


def tap_sums(padded, grad):
    images, high, wide, chans = padded.shape
    rows, cols = grad.shape[1:3]
    return pl.pallas_call(
        taps_kernel,
        grid=(chans // LANES, images),
        in_specs=[
            pl.BlockSpec((1, high, wide, LANES), lambda c, i: (i, 0, 0, c)),
            pl.BlockSpec((1, rows, cols, LANES), lambda c, i: (i, 0, 0, c)),
        ],
        out_specs=pl.BlockSpec((KERNEL * KERNEL, LANES), lambda c, i: (0, c)),
        out_shape=jax.ShapeDtypeStruct((KERNEL * KERNEL, chans), jnp.float32),
        scratch_shapes=[
            pltpu.VMEM((high, wide, LANES), jnp.float32),
            pltpu.VMEM((rows, cols, LANES), jnp.float32),
        ],
        compiler_params=pltpu.CompilerParams(vmem_limit_bytes=VMEM),
        cost_estimate=pl.CostEstimate(
            flops=10**10, bytes_accessed=2**22, transcendentals=0
        ),
    )(padded, grad)


def pad_columns(cells):
    return jnp.pad(cells, ((0, 0), (0, 0), (MARGIN, 8 - MARGIN), (0, 0)))


def depthwise(padded, kernel, height, width):
    total = jnp.zeros(padded.shape[:-3] + (height, width, padded.shape[-1]), jnp.float32)
    for row_tap in range(KERNEL):
        for col_tap in range(KERNEL):
            window = padded[:, row_tap : row_tap + height, col_tap : col_tap + width]
            total = total + window.astype(jnp.float32) * kernel[row_tap * KERNEL + col_tap]
    return total


def shards(block_input, cotangent, dw_kernel, dw_bias, ln_gain, ln_bias, w1, b1, w2, b2, gamma):
    images, rows_here, cols, chans = block_input.shape
    shard = w1.shape[1]
    pixels = images * rows_here * cols
    flat_cot = cotangent.reshape(pixels, chans).astype(jnp.float32)
    scaled = (flat_cot * gamma).astype(jnp.bfloat16)
    weights, b1_h = gather_weights(w1.T, w2, b1)
    padded = pad_columns(halo(block_input))
    scaled2 = jnp.concatenate([scaled, swap(scaled)], axis=0)
    conv = depthwise(padded, dw_kernel, rows_here, cols) + dw_bias
    center = conv - jnp.mean(conv, axis=-1, keepdims=True)
    spread = jnp.mean(center * center, axis=-1, keepdims=True)
    rstd = lax.rsqrt(spread + EPSILON).reshape(pixels, 1)
    norm = center.reshape(pixels, chans) * rstd
    normed = (norm * ln_gain + ln_bias).astype(jnp.bfloat16)
    normed2 = jnp.concatenate([normed, swap(normed)], axis=0)

    first, *parts, own, peer, sums_b1, moment_row = mlp(normed2, scaled2, weights, b1_h)
    grad_normed = own + swap(peer).astype(jnp.float32)

    weighted = grad_normed * ln_gain
    grad_conv = (
        rstd
        * (
            weighted
            - jnp.mean(weighted, axis=-1, keepdims=True)
            - norm * jnp.mean(weighted * norm, axis=-1, keepdims=True)
        )
    ).astype(jnp.bfloat16)
    grad_maps = grad_conv.reshape(block_input.shape)
    grad_padded = pad_columns(halo(grad_maps))

    grad_wide = grad_maps.astype(jnp.float32)
    cot_sums = jnp.sum(flat_cot, axis=0)
    core = lax.axis_index("core")
    y_lo = lax.axis_index("y_lo")
    sums_b1 = sums_b1[:, 0][None]
    pair_b1 = jnp.where(core == jnp.arange(2)[:, None], sums_b1, 0.0)
    local_small = jnp.concatenate(
        [
            tap_sums(padded, grad_maps),
            jnp.sum(grad_wide, axis=(0, 1, 2))[None],
            jnp.sum(grad_normed * norm, axis=0)[None],
            jnp.sum(grad_normed, axis=0)[None],
            (gamma * cot_sums)[None],
            moment_row / gamma + b2 * cot_sums,
            pair_b1.reshape(-1, chans),
            jnp.zeros((6, chans), jnp.float32),
        ],
        axis=0,
    )
    first, second, local_small = scatter_terms(first, parts, local_small)
    share, total_small, d_input = finish(
        first, second, local_small, (lambda g: transposed(g, cotangent, dw_kernel), grad_padded)
    )
    factor = 1.0 / math.sqrt(pixels * 256)
    param_grads = total_small[:54] * factor
    at = (y_lo * 8 + lax.axis_index("z")) * shard
    sums = total_small[54:58].reshape(2, -1)
    d_b1 = lax.dynamic_slice(sums, (core, at), (1, shard)).reshape(shard) * factor
    share = share * factor
    d_w1, d_w2 = share[:, :chans].T, share[:, chans:]
    return (d_input.reshape(block_input.shape), d_w1, d_b1, d_w2, param_grads)


def solution(mesh):
    fine = Mesh(mesh.devices.reshape(SIZES), AXES)
    placed = (
        P(DP, ROWS, None, None),
        P(DP, ROWS, None, None),
        P(),
        P(),
        P(),
        P(),
        P(None, DP),
        P(DP),
        P(DP, None),
        P(),
        P(),
    )
    return jax.shard_map(
        shards,
        mesh=fine,
        in_specs=placed,
        out_specs=(P(DP, ROWS, None, None), P(None, DP), P(DP), P(DP, None), P()),
        check_vma=False,
    )
```

```python
import math

import jax
import jax.numpy as jnp
import numpy as np
from jax import lax
from jax.experimental import pallas as pl
from jax.experimental.pallas import tpu as pltpu
from jax.sharding import Mesh, PartitionSpec as P

KERNEL = 7
MARGIN = 3
EPSILON = 1e-06
INV_ROOT_TWO = 0.7071067811865476
INV_ROOT_TWO_PI = 0.3989422804014327

AXES = ("y_lo", "z", "core", "y_hi", "x")
SIZES = (2, 8, 2, 2, 4)
DP = ("y_lo", "z", "core")
ROWS = ("y_hi", "x")
PAIRS = ("y_lo", "z")
Y = ("y_lo", "y_hi")


def halo(cells):
    down = [(i, i + 1) for i in range(7)]
    up = [(i + 1, i) for i in range(7)]
    above = lax.ppermute(cells[:, -MARGIN:], ROWS, down)
    below = lax.ppermute(cells[:, :MARGIN], ROWS, up)
    return jnp.concatenate([above, cells, below], axis=1)


def swap(cells):
    return lax.ppermute(cells, "core", [(0, 1), (1, 0)])


def spread_sum(part, axes):
    count = lax.axis_size(axes)
    pieces = part.reshape((count, part.shape[0] // count) + part.shape[1:])
    pieces = lax.all_to_all(pieces, axes, 0, 0)
    return jnp.sum(pieces.astype(jnp.float32), axis=0)


def gather(part, axes):
    count = lax.axis_size(axes)
    return lax.all_to_all(jnp.broadcast_to(part[None], (count,) + part.shape), axes, 0, 0)


def across(cells, m):
    flip = (m % 2) * 2 + m // 2
    return lax.ppermute(cells, Y, [(i, i ^ flip) for i in range(4)])


def gather_weights(w1_t, w2, b1):
    pair = jnp.concatenate([w1_t, w2], axis=1)
    pair = jnp.concatenate([pair, across(pair, 1)], axis=0)
    whole = lax.all_gather(pair, "z", axis=0, tiled=True)
    bias = gather(b1.astype(jnp.float32), PAIRS).reshape(2, 8, -1)
    bias = jnp.roll(bias, lax.axis_index("y_lo"), 0).transpose(1, 0, 2).reshape(-1)
    return whole, bias


def scatter_terms(first, parts, small):
    own, near, far, last = parts
    half = far.shape[0] // 2
    far = [across(across(far[:half], 1), 3), across(across(far[half:], 3), 1)]
    second = own.astype(jnp.float32) + across(near, 1).astype(jnp.float32)
    second = second + across(last, 3).astype(jnp.float32)
    second = second + jnp.concatenate(far, axis=0).astype(jnp.float32)
    first = jnp.sum(lax.all_to_all(first, "x", 0, 0).astype(jnp.float32), axis=0)
    first = first.astype(jnp.bfloat16).reshape(4, 2, 2, 48, 384)
    small = small + swap(small)
    first, second, small = lax.optimization_barrier((first, second.astype(jnp.bfloat16), small))
    second = spread_sum(second, "x")
    y_hi = lax.axis_index("y_hi")
    sent = [
        lax.dynamic_slice(
            first, (0, m % 2, y_hi ^ (m // 2), 0, 0), (4, 1, 1, 48, 384)
        ).reshape(192, 384)
        for m in range(4)
    ]
    first = sent[0].astype(jnp.float32)
    for m in (1, 2, 3):
        first = first + across(sent[m], m).astype(jnp.float32)
    return first, second, small


def two(cells):
    high = lax.reduce_precision(cells, 8, 7)
    return jnp.concatenate([high, cells - high], axis=0).astype(jnp.bfloat16)


def spread_small(small):
    x, y_hi = lax.axis_index("x"), lax.axis_index("y_hi")
    mine = lax.dynamic_slice(small, (y_hi * 32, 0), (32, 768))
    other = lax.dynamic_slice(small, ((1 - y_hi) * 32, 0), (32, 768))
    small = mine + across(mine, 1) + across(other, 2) + across(other, 3)
    total = lax.dynamic_slice(small, (x * 8, 0), (8, 768))
    for k in (1, 2, 3):
        sent = lax.dynamic_slice(small, ((x + k) % 4 * 8, 0), (8, 768))
        total = total + lax.ppermute(sent, "x", [(i, (i + k) % 4) for i in range(4)])
    return total


def finish(first, second, small, beside):
    small = spread_small(small)
    work, cells = beside
    cells, first, second, small = lax.optimization_barrier((cells, first, second, small))
    small = two(jnp.concatenate([small[:, :384], small[:, 384:]], axis=0))
    terms = jnp.concatenate([first, second], axis=0).astype(jnp.bfloat16).reshape(8, 48, 384)
    small = jnp.broadcast_to(small[None], (8,) + small.shape)
    pieces = lax.all_to_all(jnp.concatenate([terms, small], axis=1), "z", 0, 0)
    pieces, done = lax.optimization_barrier((pieces, work(cells)))
    total = jnp.sum(pieces.astype(jnp.float32), axis=0)
    small = two(total[48:64] + total[64:])
    total = gather(jnp.concatenate([total[:48].astype(jnp.bfloat16), small], axis=0), ROWS)
    total = total.astype(jnp.float32)
    share = total[:, :48].reshape(2, 4, 48, 384).transpose(0, 2, 1, 3).reshape(96, 1536)
    small = (total[:, 48:64] + total[:, 64:]).reshape(8, 2, 8, 384).transpose(0, 2, 1, 3)
    return share, small.reshape(-1, 768), done


BLOCK = 384
LANES = 128
NT = (((1,), (1,)), ((), ()))
NN = (((1,), (0,)), ((), ()))
TN = (((0,), (0,)), ((), ()))
VMEM = 56 * 2**20


def mlp_kernel(
    place, normed, scaled, w1, w2, b1, first, m0, m1, m2, m3, own, peer, d_b1, row, sums
):
    @pl.when(pl.program_id(0) == 0)
    def _():
        sums[...] = jnp.zeros_like(sums)
        row[...] = jnp.zeros_like(row)

    n, s = normed[...], scaled[...]
    step = pl.program_id(0)
    preact = lax.dot_general(w1[...], n, NT, preferred_element_type=jnp.float32) + b1[:, :1]
    cdf = 0.5 * (1.0 + lax.erf(preact * INV_ROOT_TWO))
    hidden = (preact * cdf).astype(jnp.bfloat16)
    slope = cdf + preact * jnp.exp(-0.5 * preact * preact) * INV_ROOT_TWO_PI
    grad_hidden = lax.dot_general(w2[...], s, NT, preferred_element_type=jnp.float32)
    grad_preact = (grad_hidden * slope).astype(jnp.bfloat16)
    moment = lax.dot_general(hidden, s, NN, preferred_element_type=jnp.float32)
    d_w1 = lax.dot_general(grad_preact, n, NN, preferred_element_type=jnp.float32)
    quarters = [
        half[:, at : at + 384].astype(jnp.bfloat16) for half in (d_w1, moment) for at in (0, 384)
    ]

    for two_z in range(2):

        @pl.when(step == two_z)
        def _():
            for x in range(4):
                first[x, two_z * BLOCK : (two_z + 1) * BLOCK] = quarters[x]

        for p in range(2):
            for y_hi in range(2):
                m = p + 2 * (y_hi ^ place[0])
                for k, part in enumerate((m0, m1, m2, m3)):
                    if k % 2 != p:
                        continue

                    @pl.when((step == 2 + two_z) & (m == k))
                    def _():
                        for x in range(4):
                            for z in range(2):
                                at = x * 192 + (two_z * 2 + z) * 48
                                source = z * 192 + p * 96 + y_hi * 48
                                part[at : at + 48] = quarters[x][source : source + 48]

    row[...] += jnp.sum(moment * w2[...].astype(jnp.float32), axis=0, keepdims=True)
    d_b1[...] = jnp.broadcast_to(
        jnp.sum(grad_preact.astype(jnp.float32), axis=1, keepdims=True), d_b1.shape
    )
    sums[...] += lax.dot_general(grad_preact, w1[...], TN, preferred_element_type=jnp.float32)

    @pl.when(pl.program_id(0) == pl.num_programs(0) - 1)
    def _():
        half = own.shape[0]
        own[...] = sums[:half]
        peer[...] = sums[half:].astype(jnp.bfloat16)


def mlp(normed, scaled, weights, b1):
    pixels, chans = normed.shape
    hid = weights.shape[0]
    place = lax.axis_index("y_hi").astype(jnp.int32).reshape(1)
    whole = pl.BlockSpec((pixels, chans), lambda i: (0, 0))
    half = pl.BlockSpec((pixels // 2, chans), lambda i: (0, 0))
    part = pl.BlockSpec((hid // 2, chans // 2), lambda i: (0, 0))
    lane = pl.BlockSpec((BLOCK, LANES), lambda i: (i, 0))
    return pl.pallas_call(
        mlp_kernel,
        grid=(hid // BLOCK,),
        in_specs=[
            pl.BlockSpec(memory_space=pltpu.SMEM),
            whole,
            whole,
            pl.BlockSpec((BLOCK, chans), lambda i: (i, 0)),
            pl.BlockSpec((BLOCK, chans), lambda i: (i, 1)),
            lane,
        ],
        out_specs=[
            pl.BlockSpec((4, hid // 2, chans // 2), lambda i: (0, 0, 0)),
            part,
            part,
            part,
            part,
            half,
            half,
            lane,
            pl.BlockSpec((1, chans), lambda i: (0, 0)),
        ],
        out_shape=[jax.ShapeDtypeStruct((4, hid // 2, chans // 2), jnp.bfloat16)]
        + [jax.ShapeDtypeStruct((hid // 2, chans // 2), jnp.bfloat16)] * 4
        + [
            jax.ShapeDtypeStruct((pixels // 2, chans), jnp.float32),
            jax.ShapeDtypeStruct((pixels // 2, chans), jnp.bfloat16),
            jax.ShapeDtypeStruct((hid, LANES), jnp.float32),
            jax.ShapeDtypeStruct((1, chans), jnp.float32),
        ],
        scratch_shapes=[pltpu.VMEM((pixels, chans), jnp.float32)],
        compiler_params=pltpu.CompilerParams(vmem_limit_bytes=VMEM),
        cost_estimate=pl.CostEstimate(
            flops=10 * pixels * hid * chans, bytes_accessed=2**24, transcendentals=2 * pixels * hid
        ),
    )(place, normed, scaled, weights, weights, jnp.broadcast_to(b1[:, None], (hid, LANES)))


def transposed_kernel(padded, cotangent, kernel, d_input, wide):
    rows, cols = d_input.shape[1:3]
    wide[...] = padded[0].astype(jnp.float32)
    for at in range(0, cols, 24):
        sums = [cotangent[0, r, at : at + 24].astype(jnp.float32) for r in range(rows)]
        for b in range(KERNEL):
            column = [(KERNEL - 1 - a) * KERNEL + KERNEL - 1 - b for a in range(KERNEL)]
            taps = [kernel[t : t + 1] for t in column]
            for r in range(rows + KERNEL - 1):
                cells = wide[r, at + b : at + b + 24]
                for a in range(max(0, r - rows + 1), min(KERNEL, r + 1)):
                    sums[r - a] = sums[r - a] + cells * taps[a]
        for r in range(rows):
            d_input[0, r, at : at + 24] = sums[r].astype(jnp.bfloat16)


def transposed(padded, cotangent, kernel):
    images, high, wide, chans = padded.shape
    rows, cols = cotangent.shape[1:3]
    maps = pl.BlockSpec((1, rows, cols, LANES), lambda c, i: (i, 0, 0, c))
    return pl.pallas_call(
        transposed_kernel,
        grid=(chans // LANES, images),
        in_specs=[
            pl.BlockSpec((1, high, wide, LANES), lambda c, i: (i, 0, 0, c)),
            maps,
            pl.BlockSpec((KERNEL * KERNEL, LANES), lambda c, i: (0, c)),
        ],
        out_specs=maps,
        out_shape=jax.ShapeDtypeStruct(cotangent.shape, jnp.bfloat16),
        scratch_shapes=[pltpu.VMEM((high, wide, LANES), jnp.float32)],
        compiler_params=pltpu.CompilerParams(vmem_limit_bytes=VMEM),
        cost_estimate=pl.CostEstimate(
            flops=10**10, bytes_accessed=2**22, transcendentals=0
        ),
    )(padded, cotangent, kernel)


def taps_kernel(padded, grad, sums, wide, grad_wide):
    rows, cols = grad.shape[1:3]
    wide[...] = padded[0].astype(jnp.float32)
    grad_wide[...] = grad[0].astype(jnp.float32)

    @pl.when(pl.program_id(1) == 0)
    def _():
        sums[...] = jnp.zeros_like(sums)

    for b in range(KERNEL):
        totals = [jnp.zeros((8, LANES), jnp.float32) for _ in range(KERNEL)]
        for at in range(0, cols, 16):
            own = [grad_wide[r, at : at + 16] for r in range(rows)]
            for r in range(rows + KERNEL - 1):
                cells = wide[r, at + b : at + b + 16]
                for a in range(max(0, r - rows + 1), min(KERNEL, r + 1)):
                    product = cells * own[r - a]
                    totals[a] = totals[a] + (product[:8] + product[8:])
        for a in range(KERNEL):
            t = a * KERNEL + b
            sums[t : t + 1] += jnp.sum(totals[a], axis=0, keepdims=True)


def tap_sums(padded, grad):
    images, high, wide, chans = padded.shape
    rows, cols = grad.shape[1:3]
    return pl.pallas_call(
        taps_kernel,
        grid=(chans // LANES, images),
        in_specs=[
            pl.BlockSpec((1, high, wide, LANES), lambda c, i: (i, 0, 0, c)),
            pl.BlockSpec((1, rows, cols, LANES), lambda c, i: (i, 0, 0, c)),
        ],
        out_specs=pl.BlockSpec((KERNEL * KERNEL, LANES), lambda c, i: (0, c)),
        out_shape=jax.ShapeDtypeStruct((KERNEL * KERNEL, chans), jnp.float32),
        scratch_shapes=[
            pltpu.VMEM((high, wide, LANES), jnp.float32),
            pltpu.VMEM((rows, cols, LANES), jnp.float32),
        ],
        compiler_params=pltpu.CompilerParams(vmem_limit_bytes=VMEM),
        cost_estimate=pl.CostEstimate(
            flops=10**10, bytes_accessed=2**22, transcendentals=0
        ),
    )(padded, grad)


def pad_columns(cells):
    return jnp.pad(cells, ((0, 0), (0, 0), (MARGIN, 8 - MARGIN), (0, 0)))


def depthwise(padded, kernel, height, width):
    total = jnp.zeros(padded.shape[:-3] + (height, width, padded.shape[-1]), jnp.float32)
    for row_tap in range(KERNEL):
        for col_tap in range(KERNEL):
            window = padded[:, row_tap : row_tap + height, col_tap : col_tap + width]
            total = total + window.astype(jnp.float32) * kernel[row_tap * KERNEL + col_tap]
    return total


def shards(block_input, cotangent, dw_kernel, dw_bias, ln_gain, ln_bias, w1, b1, w2, b2, gamma):
    images, rows_here, cols, chans = block_input.shape
    shard = w1.shape[1]
    pixels = images * rows_here * cols
    flat_cot = cotangent.reshape(pixels, chans).astype(jnp.float32)
    scaled = (flat_cot * gamma).astype(jnp.bfloat16)
    weights, b1_h = gather_weights(w1.T, w2, b1)
    padded = pad_columns(halo(block_input))
    scaled2 = jnp.concatenate([scaled, swap(scaled)], axis=0)
    conv = depthwise(padded, dw_kernel, rows_here, cols) + dw_bias
    center = conv - jnp.mean(conv, axis=-1, keepdims=True)
    spread = jnp.mean(center * center, axis=-1, keepdims=True)
    rstd = lax.rsqrt(spread + EPSILON).reshape(pixels, 1)
    norm = center.reshape(pixels, chans) * rstd
    normed = (norm * ln_gain + ln_bias).astype(jnp.bfloat16)
    normed2 = jnp.concatenate([normed, swap(normed)], axis=0)

    first, *parts, own, peer, sums_b1, moment_row = mlp(normed2, scaled2, weights, b1_h)
    grad_normed = own + swap(peer).astype(jnp.float32)

    weighted = grad_normed * ln_gain
    grad_conv = (
        rstd
        * (
            weighted
            - jnp.mean(weighted, axis=-1, keepdims=True)
            - norm * jnp.mean(weighted * norm, axis=-1, keepdims=True)
        )
    ).astype(jnp.bfloat16)
    grad_maps = grad_conv.reshape(block_input.shape)
    grad_padded = pad_columns(halo(grad_maps))

    grad_wide = grad_maps.astype(jnp.float32)
    cot_sums = jnp.sum(flat_cot, axis=0)
    core = lax.axis_index("core")
    y_lo = lax.axis_index("y_lo")
    sums_b1 = jnp.roll(sums_b1[:, 0].reshape(8, 2, shard), y_lo, 1)
    sums_b1 = sums_b1.transpose(1, 0, 2).reshape(1, -1)
    pair_b1 = jnp.where(core == jnp.arange(2)[:, None], sums_b1, 0.0)
    local_small = jnp.concatenate(
        [
            tap_sums(padded, grad_maps),
            jnp.sum(grad_wide, axis=(0, 1, 2))[None],
            jnp.sum(grad_normed * norm, axis=0)[None],
            jnp.sum(grad_normed, axis=0)[None],
            (gamma * cot_sums)[None],
            moment_row / gamma + b2 * cot_sums,
            pair_b1.reshape(-1, chans),
            jnp.zeros((6, chans), jnp.float32),
        ],
        axis=0,
    )
    first, second, local_small = scatter_terms(first, parts, local_small)
    share, total_small, d_input = finish(
        first, second, local_small, (lambda g: transposed(g, cotangent, dw_kernel), grad_padded)
    )
    factor = 1.0 / math.sqrt(pixels * 256)
    param_grads = total_small[:54] * factor
    at = (y_lo * 8 + lax.axis_index("z")) * shard
    sums = total_small[54:58].reshape(2, -1)
    d_b1 = lax.dynamic_slice(sums, (core, at), (1, shard)).reshape(shard) * factor
    share = share * factor
    d_w1, d_w2 = share[:, :chans].T, share[:, chans:]
    return (d_input.reshape(block_input.shape), d_w1, d_b1, d_w2, param_grads)


def solution(mesh):
    fine = Mesh(mesh.devices.reshape(SIZES), AXES)
    placed = (
        P(DP, ROWS, None, None),
        P(DP, ROWS, None, None),
        P(),
        P(),
        P(),
        P(),
        P(None, DP),
        P(DP),
        P(DP, None),
        P(),
        P(),
    )
    return jax.shard_map(
        shards,
        mesh=fine,
        in_specs=placed,
        out_specs=(P(DP, ROWS, None, None), P(None, DP), P(DP), P(DP, None), P()),
        check_vma=False,
    )
```
